512 devices in a mesh: blk: 64 (over z, y_lo, core), member: 8 (over x, y_hi).
Axes of the slice: x: 4, y: 4 (y_hi: 2, y_lo: 2; y = y_hi * 2 + y_lo), z: 16, core: 2. Of those that a mesh axis runs over, the one named last changes fastest.
Arguments:
- images: bfloat16 [65536, 1152], P(('blk', 'member')), may hold values from -2.5 to 2.5
- texts: bfloat16 [65536, 1152], P(('blk', 'member')), may hold values from -2.5 to 2.5
- log_scale: float32 [1], replicated, may hold values from 2 to 2.6
- bias: float32 [1], replicated, may hold values from -6 to -4
Outputs:
- image_grad: float32 [65536, 1152], P(('blk', 'member'))
- text_grad: float32 [65536, 1152], P(('blk', 'member'))
- text_loss: float32 [65536], P(('blk', 'member'))
The draws below stay inside these ranges and needn't reach their ends.
All inputs are finite; a program needn't handle non-finite values.
Results may differ from the reference program's by a relative error of at most 0.02.
Values may be sent and summed in bfloat16 or wider, within the bound.
A program may use at most 64 MiB of HBM per device.

```python
import math
import jax
import jax.numpy as jnp
from jax import lax

D = 1152
PAIRS_DEV = 128
STEPS = 8
BATCH = 65536
N_BLK = 64
N_MEMBER = 8


def shared_part(key):
    keys = jax.random.split(key, 1)
    base = jnp.clip(jax.random.normal(keys[0], (BATCH, D), jnp.float32), -5.0, 5.0)
    return base


def spread(key, count, low, high):
    return jnp.exp(jax.random.uniform(key, (count, 1), jnp.float32, math.log(low), math.log(high)))


def draw_images(key, part):
    shared = shared_part(key)
    key = jax.random.fold_in(key, 3)
    keys = jax.random.split(key, 2)
    row_scale = spread(keys[0], BATCH, 0.3, 3.0)
    col_scale = spread(keys[1], D, 0.3, 3.0).reshape(1, D)
    values = shared * row_scale * col_scale / math.sqrt(D)
    return jnp.clip(values, -2.5, 2.5).astype(jnp.bfloat16)


def draw_texts(key, part):
    shared = shared_part(key)
    key = jax.random.fold_in(key, 7)
    keys = jax.random.split(key, 3)
    own = jnp.clip(jax.random.normal(keys[0], (BATCH, D), jnp.float32), -5.0, 5.0)
    mixed = 0.75 * shared + 0.66 * own
    row_scale = spread(keys[1], BATCH, 0.3, 3.0)
    col_scale = spread(keys[2], D, 0.3, 3.0).reshape(1, D)
    values = mixed * row_scale * col_scale / math.sqrt(D)
    return jnp.clip(values, -2.5, 2.5).astype(jnp.bfloat16)


def setup_inputs(seed: int = 0) -> dict:
    key_of = jax.random.split(jax.random.key(seed), 5)
    images = draw_images(jax.random.fold_in(key_of[4], 71), 0)
    texts = draw_texts(jax.random.fold_in(key_of[4], 71), 0)
    log_scale = jnp.clip(jax.random.uniform(key_of[2], (1,), jnp.float32, 2.0, 2.6), 2.0, 2.6)
    bias = jnp.clip(jax.random.uniform(key_of[3], (1,), jnp.float32, -6.0, -4.0), -6.0, -4.0)
    return {"images": images, "texts": texts, "log_scale": log_scale, "bias": bias}


def normalize(values):
    wide = values.astype(jnp.float32)
    inverse = lax.rsqrt(lax.optimization_barrier(jnp.sum(wide * wide, axis=-1, keepdims=True)) + 1e-06)
    return (wide * inverse, inverse)

def chain_back(unit, inverse, upstream):
    return inverse * (upstream - unit * lax.optimization_barrier(jnp.sum(unit * upstream, axis=-1, keepdims=True)))

def reference(images, texts, log_scale, bias):
    temper = jnp.exp(log_scale[0])
    offset = bias[0]
    image_unit, image_inv = normalize(images)
    text_unit, text_inv = normalize(texts)
    image_low = lax.optimization_barrier(image_unit.astype(jnp.bfloat16)).astype(jnp.float32)
    text_low = lax.optimization_barrier(text_unit.astype(jnp.bfloat16)).astype(jnp.float32)
    blocks = N_BLK
    group = PAIRS_DEV * N_MEMBER
    image_blocks = image_low.reshape(blocks, group, D)
    text_blocks = text_low.reshape(blocks, N_MEMBER, PAIRS_DEV, D)
    row_ids = jnp.arange(group, dtype=jnp.int32)
    image_sum = jnp.zeros((blocks, group, D), jnp.float32)
    grad_parts = []
    loss_parts = []
    for member in range(N_MEMBER):
        own_cols = member * PAIRS_DEV + jnp.arange(PAIRS_DEV, dtype=jnp.int32)
        matched = (row_ids[:, None] == own_cols[None, :]).astype(jnp.float32)
        own_texts = text_blocks[:, member]
        partial_value = jnp.zeros((blocks, group, D), jnp.float32)
        member_grad = jnp.zeros((blocks, PAIRS_DEV, D), jnp.float32)
        member_loss = jnp.zeros((blocks, PAIRS_DEV), jnp.float32)
        for step in range(STEPS):
            visiting = jnp.roll(own_texts, step, axis=0)
            logits = temper * jnp.einsum('bid,bjd->bij', image_blocks, visiting) + offset
            probs = jax.nn.sigmoid(logits)
            pair_loss = jax.nn.softplus(logits)
            if step == 0:
                probs = probs - matched[None]
                pair_loss = pair_loss - matched[None] * logits
            slope = lax.optimization_barrier(probs.astype(jnp.bfloat16)).astype(jnp.float32)
            partial_value = partial_value + jnp.einsum('bij,bjd->bid', slope, visiting)
            back = jnp.einsum('bij,bid->bjd', slope, image_blocks)
            member_grad = member_grad + jnp.roll(back, -step, axis=0)
            member_loss = member_loss + jnp.roll(lax.optimization_barrier(jnp.sum(pair_loss, axis=1)), -step, axis=0)
        image_sum = image_sum + lax.optimization_barrier(partial_value.astype(jnp.bfloat16)).astype(jnp.float32)
        grad_parts.append(member_grad)
        loss_parts.append(member_loss)
    text_sum = jnp.stack(grad_parts, axis=1).reshape(BATCH, D)
    text_loss = jnp.stack(loss_parts, axis=1).reshape(BATCH) / STEPS
    image_grad = chain_back(image_unit, image_inv, temper * image_sum.reshape(BATCH, D))
    text_grad = chain_back(text_unit, text_inv, temper * text_sum)
    return (image_grad, text_grad, text_loss)
```

```python
import jax
import jax.numpy as jnp
from jax import lax
from jax.experimental import pallas as pl
from jax.experimental.pallas import tpu as pltpu
from jax.sharding import PartitionSpec as P

STEPS = 8
B = 128
HALF = B // 2
MESH = pl.DeviceIdType.MESH

OWN, XM, XP, Y, YXM, YXP, X2, YX2 = range(8)
T0B, T0A, T1A, T2A, T3A, T1B, T2B, T3B, RELAY = range(9)
G1A, G1B, G2A, G2B, G3A, G3B, GR, GS = range(8)


def normalized(ref):
    wide = ref[...].astype(jnp.float32)
    inverse = lax.rsqrt(jnp.sum(wide * wide, axis=-1, keepdims=True) + 1e-06)
    return wide * inverse, inverse


def chain_back(unit, inverse, upstream):
    return inverse * (upstream - unit * jnp.sum(unit * upstream, axis=-1, keepdims=True))


def kernel(
    images, texts, log_scale, bias, image_grad, text_grad, text_loss,
    img, txt, pg, tgr, loss, sp, rxh, rx, sg, rg, sl, rl, ssem, rsem,
):
    blk, member = lax.axis_index("blk"), lax.axis_index("member")
    n_blk, n_member = lax.axis_size("blk"), lax.axis_size("member")
    core = blk % 2
    y_lo = (blk // 2) % 2
    at_core = (blk + 1 - 2 * core, member)
    at_pair = (blk + 2 - 4 * y_lo, member)
    at_zp = ((blk + 4) % n_blk, member)
    at_zm = ((blk + n_blk - 4) % n_blk, member)
    at_xp = (blk, (member + 2) % n_member)
    at_xm = (blk, (member + n_member - 2) % n_member)
    at_y = (blk, member + 1 - 2 * (member % 2))

    barrier = pltpu.get_barrier_semaphore()
    partners = (at_core, at_pair, at_zp, at_zm, at_xp, at_xm, at_y)
    for device in partners:
        pl.semaphore_signal(barrier, inc=1, device_id=device, device_id_type=MESH)

    used = [0]
    sent = []

    def copies(src, src_row, dst, dst_row, rows, device, pieces=1, other=None):
        out = []
        step = rows // pieces
        for k in range(pieces):
            s = used[0]
            used[0] += 1
            made = [
                pltpu.make_async_remote_copy(
                    src_ref=a.at[pl.ds(r + k * step, step)],
                    dst_ref=dst.at[pl.ds(dst_row + k * step, step)],
                    send_sem=ssem.at[s],
                    recv_sem=rsem.at[s],
                    device_id=device,
                    device_id_type=MESH,
                )
                for a, r in [(src, src_row)] + ([other] if other else [])
            ]
            sent.append(made[0])
            out.append(made if other else made[0])
        return out

    f_xp = copies(img, OWN * B, img, XM * B, B, at_xp, 2)
    f_xm = copies(img, OWN * B, img, XP * B, B, at_xm, 2)
    f_y = copies(img, OWN * B, img, Y * B, B, at_y, 2)
    f_x2t = copies(img, XM * B, img, X2 * B, HALF, at_xp)
    f_x2b = copies(img, XP * B + HALF, img, X2 * B + HALF, HALF, at_xm)
    f_yxp = copies(img, Y * B, img, YXM * B, B, at_xp, 2)
    f_yxm = copies(img, Y * B, img, YXP * B, B, at_xm, 2)
    f_yx2t = copies(img, YXM * B, img, YX2 * B, HALF, at_xp)
    f_yx2b = copies(img, YXP * B + HALF, img, YX2 * B + HALF, HALF, at_xm)
    f_z1 = copies(txt, T0B * B, txt, T0A * B, B, at_zp, 2)
    f_z2 = copies(txt, T0A * B, txt, RELAY * B, B, at_zp, 2)
    f_c1a = copies(txt, T0A * B, txt, T1A * B, B, at_core)
    f_c1b = copies(txt, T0B * B, txt, T1B * B, B, at_core, 2, (txt, RELAY * B))
    f_p2a = copies(txt, T0A * B, txt, T2A * B, B, at_pair, 2)
    f_p2b = copies(txt, T0B * B, txt, T2B * B, B, at_pair, 2, (txt, RELAY * B))
    f_c3a = copies(txt, T2A * B, txt, T3A * B, B, at_core)
    f_c3b = copies(txt, T2B * B, txt, T3B * B, B, at_core)
    b_7t = copies(sp, YX2 * B, rxh, 0, HALF, at_xm)
    b_7b = copies(sp, YX2 * B + HALF, rxh, HALF, HALF, at_xp)
    b_6t = copies(sp, X2 * B, rxh, 2 * HALF, HALF, at_xm)
    b_6b = copies(sp, X2 * B + HALF, rxh, 3 * HALF, HALF, at_xp)
    b_4 = copies(sp, YXM * B, rx, 0 * B, B, at_xm, 2)
    b_5 = copies(sp, YXP * B, rx, 1 * B, B, at_xp, 2)
    b_1 = copies(sp, XM * B, rx, 2 * B, B, at_xm, 2)
    b_2 = copies(sp, XP * B, rx, 3 * B, B, at_xp, 2)
    b_3 = copies(sp, Y * B, rx, 4 * B, B, at_y, 2)
    b_c3a = copies(sg, G3A * B, rg, G3A * B, B, at_core)
    b_c3b = copies(sg, G3B * B, rg, G3B * B, B, at_core)
    b_c1 = copies(sg, G1A * B, rg, G1A * B, 2 * B, at_core)
    b_p2b = copies(sg, G2B * B, rg, G2B * B, B, at_pair, 2)
    b_p2a = copies(sg, G2A * B, rg, G2A * B, B, at_pair, 2)
    b_zr = copies(sg, GR * B, rg, GR * B, B, at_zm, 2)
    b_zs = copies(sg, GS * B, rg, GS * B, B, at_zm, 2)
    l_c = copies(sl, 0, rl, 0, 8, at_core)
    l_p = copies(sl, 8, rl, 8, 8, at_pair)
    l_zr = copies(sl, 16, rl, 16, 8, at_zm)
    l_zs = copies(sl, 24, rl, 24, 8, at_zm)

    def start(*lists):
        for group in lists:
            for c in group:
                c.start()

    def landed(*lists):
        for group in lists:
            for c in group:
                (c[0] if isinstance(c, list) else c).wait_recv()

    def start_choice(group, which):
        for c in group:
            c[which].start()

    temper = jnp.exp(jnp.full((1, B), log_scale[0], jnp.float32))
    offset = bias[0]

    unit, _ = normalized(images)
    img[pl.ds(OWN * B, B), :] = unit.astype(jnp.bfloat16)
    unit, _ = normalized(texts)
    txt[pl.ds(T0B * B, B), :] = unit.astype(jnp.bfloat16)

    pl.semaphore_wait(barrier, len(partners))

    start(f_y, f_xp, f_xm, f_z1)

    @pl.when(core == 0)
    def _():
        start_choice(f_c1b, 0)

    @pl.when(y_lo == 0)
    def _():
        start_choice(f_p2b, 0)

    pg[...] = jnp.zeros_like(pg)
    tgr[...] = jnp.zeros_like(tgr)
    loss[...] = jnp.zeros_like(loss)

    def tile(row, rows, first, blocks, diagonal=False):
        cols = blocks * B
        i = img[pl.ds(row, rows), :]
        t = txt[pl.ds(first * B, cols), :]
        scale = jnp.concatenate([temper] * blocks, axis=1)
        logits = (
            lax.dot_general(i, t, (((1,), (1,)), ((), ())), preferred_element_type=jnp.float32)
            * scale
            + offset
        )
        grown = jnp.exp(logits)
        slope = grown * pl.reciprocal(1.0 + grown, approx=True)
        part = rows
        while part > rows // 8:
            part //= 2
            grown = grown[:part] + grown[part:] + grown[:part] * grown[part:]
        logs = jnp.where(
            grown < 0.0078125,
            grown * (1.0 - grown * (0.5 - grown * (1.0 / 3.0))),
            jnp.log(1.0 + grown),
        )
        column = jnp.sum(logs, axis=0, keepdims=True)
        if diagonal:
            at_row = row + lax.broadcasted_iota(jnp.int32, (rows, cols), 0)
            at_col = first * B + lax.broadcasted_iota(jnp.int32, (rows, cols), 1)
            matched = jnp.logical_and(at_row == at_col, at_col < B)
            slope = slope - jnp.where(matched, 1.0, 0.0)
            column = column - jnp.sum(jnp.where(matched, logits, 0.0), axis=0, keepdims=True)
        for k in range(blocks):
            loss[pl.ds(first + k, 1), :] += column[:, k * B : (k + 1) * B]
        low = slope.astype(jnp.bfloat16)
        pg[pl.ds(row, rows), :] += jnp.dot(low, t, preferred_element_type=jnp.float32)
        tgr[pl.ds(first * B, cols), :] += lax.dot_general(
            low, i, (((0,), (0,)), ((), ())), preferred_element_type=jnp.float32
        )

    def tiles(first_slot, slots, first, blocks, diagonal=False):
        def body(k, carry):
            row = pl.multiple_of((first_slot + 2 * k) * B, 2 * B)
            tile(row, 2 * B, first, blocks, diagonal)
            return carry

        lax.fori_loop(0, slots // 2, body, 0)

    landed(f_y)
    start(f_yxp, f_yxm)
    landed(f_xp, f_xm)
    start(f_x2t, f_x2b)
    landed(f_z1)
    start(f_z2, f_p2a, f_c1a)
    tiles(OWN, 4, T0B, 2, diagonal=True)
    landed(f_p2a)
    start(f_c3a)
    landed(f_z2)

    @pl.when(core == 1)
    def _():
        start_choice(f_c1b, 1)

    @pl.when(y_lo == 1)
    def _():
        start_choice(f_p2b, 1)

    landed(f_c1a, f_c3a, f_c1b)
    landed(f_yxp, f_yxm)
    start(f_yx2t, f_yx2b)
    tiles(OWN, 4, T1A, 4)
    tiles(YXM, 2, T0B, 6)
    landed(f_p2b)
    start(f_c3b)
    landed(f_c3b, f_x2t, f_x2b, f_yx2t, f_yx2b)
    tiles(X2, 2, T0B, 8)

    def stage(slot):
        sp[pl.ds(slot * B, B), :] = pg[pl.ds(slot * B, B), :].astype(jnp.bfloat16)

    stage(YX2)
    start(b_7t, b_7b)
    stage(X2)
    start(b_6t, b_6b)
    tiles(OWN, 6, T2B, 2)

    def text_sum(slot):
        return tgr[pl.ds(slot * B, B), :]

    def put(slot, value):
        sg[pl.ds(slot * B, B), :] = value.astype(jnp.bfloat16)

    def got(slot):
        return rg[pl.ds(slot * B, B), :].astype(jnp.float32)

    put(G3B, text_sum(T3B))
    start(b_c3b)
    put(G3A, text_sum(T3A))
    start(b_c3a)
    sl[pl.ds(0, 8), :] = loss[...]
    start(l_c)

    def pass_on(slot, top, half):
        add = HALF * half
        mine = pg[pl.ds(slot * B + (0 if top else HALF), HALF), :]
        total = mine + rxh[pl.ds(add, HALF), :].astype(jnp.float32)
        rest = slot * B + (HALF if top else 0)
        sp[pl.ds(rest, HALF), :] = pg[pl.ds(rest, HALF), :].astype(jnp.bfloat16)
        sp[pl.ds(slot * B + (0 if top else HALF), HALF), :] = total.astype(jnp.bfloat16)

    landed(b_7t, b_7b)
    pass_on(YXM, True, 0)
    start(b_4)
    pass_on(YXP, False, 1)
    start(b_5)

    landed(b_c3b)
    put(G2B, text_sum(T2B) + got(G3B))
    start(b_p2b)
    landed(b_c3a)
    put(G2A, text_sum(T2A) + got(G3A))
    start(b_p2a)
    put(G1A, text_sum(T1A))
    put(G1B, text_sum(T1B))
    start(b_c1)
    landed(l_c)
    loss_2a = loss[pl.ds(T2A, 1), :] + rl[pl.ds(T3A, 1), :]
    loss_2b = loss[pl.ds(T2B, 1), :] + rl[pl.ds(T3B, 1), :]
    sl[pl.ds(8, 8), :] = jnp.concatenate([loss_2a, loss_2b] * 4, axis=0)
    start(l_p)

    landed(b_6t, b_6b)
    pass_on(XM, True, 2)
    start(b_1)
    pass_on(XP, False, 3)
    start(b_2)

    odd = core.astype(jnp.float32)
    high = y_lo.astype(jnp.float32)
    landed(b_c1, b_p2b)
    put(GR, got(G1B) * odd + got(G2B) * high)
    start(b_zr)
    landed(l_p)
    sl[pl.ds(16, 8), :] = jnp.broadcast_to(
        rl[pl.ds(T1B, 1), :] * odd + rl[pl.ds(9, 1), :] * high, (8, B)
    )
    start(l_zr)

    landed(b_4, b_5)
    sp[pl.ds(Y * B, B), :] = (
        pg[pl.ds(Y * B, B), :]
        + rx[pl.ds(0 * B, B), :].astype(jnp.float32)
        + rx[pl.ds(1 * B, B), :].astype(jnp.float32)
    ).astype(jnp.bfloat16)
    start(b_3)

    landed(b_p2a)
    landed(b_zr)
    put(GS, text_sum(T0A) + got(G1A) + got(G2A) + got(GR))
    start(b_zs)
    landed(l_zr)
    sl[pl.ds(24, 8), :] = jnp.broadcast_to(
        loss[pl.ds(T0A, 1), :] + rl[pl.ds(T1A, 1), :] + rl[pl.ds(8, 1), :] + rl[pl.ds(16, 1), :], (8, B)
    )
    start(l_zs)

    wide_temper = jnp.concatenate([temper] * (images.shape[1] // B), axis=1)

    landed(b_1, b_2, b_3)
    image_sum = (
        pg[pl.ds(OWN * B, B), :]
        + rx[pl.ds(2 * B, B), :].astype(jnp.float32)
        + rx[pl.ds(3 * B, B), :].astype(jnp.float32)
        + rx[pl.ds(4 * B, B), :].astype(jnp.float32)
    )
    unit, inverse = normalized(images)
    image_grad[...] = chain_back(unit, inverse, wide_temper * image_sum)

    landed(b_zs, l_zs)
    own_sum = (
        text_sum(T0B) + got(G1B) * (1.0 - odd) + got(G2B) * (1.0 - high) + got(GS)
    )
    unit, inverse = normalized(texts)
    text_grad[...] = chain_back(unit, inverse, wide_temper * own_sum)
    text_loss[...] = (
        loss[pl.ds(T0B, 1), :]
        + rl[pl.ds(T1B, 1), :] * (1.0 - odd)
        + rl[pl.ds(9, 1), :] * (1.0 - high)
        + rl[pl.ds(24, 1), :]
    ) * (1.0 / STEPS)
    for c in sent:
        c.wait_send()


SEMS = 80


def on_device(images, texts, log_scale, bias):
    width = images.shape[1]
    rows = lambda n, dtype: pltpu.VMEM((n, width), dtype)
    vmem = pl.BlockSpec(memory_space=pltpu.VMEM)
    smem = pl.BlockSpec(memory_space=pltpu.SMEM)
    image_grad, text_grad, text_loss = pl.pallas_call(
        kernel,
        out_shape=(
            jax.ShapeDtypeStruct((B, width), jnp.float32),
            jax.ShapeDtypeStruct((B, width), jnp.float32),
            jax.ShapeDtypeStruct((1, B), jnp.float32),
        ),
        in_specs=[vmem, vmem, smem, smem],
        out_specs=(vmem, vmem, vmem),
        scratch_shapes=[
            rows(8 * B, jnp.bfloat16),
            rows(9 * B, jnp.bfloat16),
            rows(8 * B, jnp.float32),
            rows(8 * B, jnp.float32),
            pltpu.VMEM((8, B), jnp.float32),
            rows(8 * B, jnp.bfloat16),
            rows(4 * HALF, jnp.bfloat16),
            rows(5 * B, jnp.bfloat16),
            rows(8 * B, jnp.bfloat16),
            rows(8 * B, jnp.bfloat16),
            pltpu.VMEM((32, B), jnp.float32),
            pltpu.VMEM((32, B), jnp.float32),
            pltpu.SemaphoreType.DMA((SEMS,)),
            pltpu.SemaphoreType.DMA((SEMS,)),
        ],
        compiler_params=pltpu.CompilerParams(
            collective_id=0, has_side_effects=True, vmem_limit_bytes=52 << 20
        ),
        name="window",
    )(images, texts, log_scale, bias)
    return image_grad, text_grad, text_loss.reshape(B)


def solution(mesh):
    return jax.shard_map(
        on_device,
        mesh=mesh,
        in_specs=(P(("blk", "member"), None), P(("blk", "member"), None), P(), P()),
        out_specs=(P(("blk", "member"), None), P(("blk", "member"), None), P(("blk", "member"))),
        check_vma=False,
    )
```

```python
import jax
import jax.numpy as jnp
from jax import lax
from jax.experimental import pallas as pl
from jax.experimental.pallas import tpu as pltpu
from jax.sharding import PartitionSpec as P

STEPS = 8
B = 128
HALF = B // 2
MESH = pl.DeviceIdType.MESH

OWN, XM, XP, Y, YXM, YXP, X2, YX2 = range(8)
T0B, T0A, T1A, T2F, T3F, T1B, T2L, T3L, RELAY = range(9)
G1A, G1B, G2F, G2L, G3F, G3L, GR, GS = range(8)


def normalized(ref):
    wide = ref[...].astype(jnp.float32)
    inverse = lax.rsqrt(jnp.sum(wide * wide, axis=-1, keepdims=True) + 1e-06)
    return wide * inverse, inverse


def chain_back(unit, inverse, upstream):
    return inverse * (upstream - unit * jnp.sum(unit * upstream, axis=-1, keepdims=True))


def kernel(
    images_in, texts_in, log_scale, bias, image_grad, text_grad, text_loss,
    images, texts, img, txt, pg, tgr, loss, sp, rxh, rx, sg, rg, sl, rl, isem, ssem, rsem,
):
    blk, member = lax.axis_index("blk"), lax.axis_index("member")
    n_blk, n_member = lax.axis_size("blk"), lax.axis_size("member")
    core = blk % 2
    y_lo = (blk // 2) % 2
    at_core = (blk + 1 - 2 * core, member)
    at_pair = (blk + 2 - 4 * y_lo, member)
    at_zp = ((blk + 4) % n_blk, member)
    at_zm = ((blk + n_blk - 4) % n_blk, member)
    at_xp = (blk, (member + 2) % n_member)
    at_xm = (blk, (member + n_member - 2) % n_member)
    at_y = (blk, member + 1 - 2 * (member % 2))

    image_load = pltpu.make_async_copy(images_in, images, isem.at[0])
    text_load = pltpu.make_async_copy(texts_in, texts, isem.at[1])
    image_load.start()
    text_load.start()

    barrier = pltpu.get_barrier_semaphore()
    partners = (at_core, at_pair, at_zp, at_zm, at_xp, at_xm, at_y)
    for device in partners:
        pl.semaphore_signal(barrier, inc=1, device_id=device, device_id_type=MESH)

    used = [0]
    sent = []

    def copies(src, src_row, dst, dst_row, rows, device, pieces=1, other=None):
        out = []
        step = rows // pieces
        for k in range(pieces):
            s = used[0]
            used[0] += 1
            made = [
                pltpu.make_async_remote_copy(
                    src_ref=a.at[pl.ds(r + k * step, step)],
                    dst_ref=dst.at[pl.ds(dst_row + k * step, step)],
                    send_sem=ssem.at[s],
                    recv_sem=rsem.at[s],
                    device_id=device,
                    device_id_type=MESH,
                )
                for a, r in [(src, src_row)] + ([other] if other else [])
            ]
            sent.append(made[0])
            out.append(made if other else made[0])
        return out

    f_xp = copies(img, OWN * B, img, XM * B, B, at_xp, 2)
    f_xm = copies(img, OWN * B, img, XP * B, B, at_xm, 2)
    f_y = copies(img, OWN * B, img, Y * B, B, at_y, 2)
    f_x2t = copies(img, XM * B, img, X2 * B, HALF, at_xp)
    f_x2b = copies(img, XP * B + HALF, img, X2 * B + HALF, HALF, at_xm)
    f_yxp = copies(img, Y * B, img, YXM * B, B, at_xp, 2)
    f_yxm = copies(img, Y * B, img, YXP * B, B, at_xm, 2)
    f_yx2t = copies(img, YXM * B, img, YX2 * B, HALF, at_xp)
    f_yx2b = copies(img, YXP * B + HALF, img, YX2 * B + HALF, HALF, at_xm)
    f_z1 = copies(txt, T0B * B, txt, T0A * B, B, at_zp, 2)
    f_z2 = copies(txt, T0A * B, txt, RELAY * B, B, at_zp, 2)
    f_c1a = copies(txt, T0A * B, txt, T1A * B, B, at_core)
    f_c1b = copies(txt, T0B * B, txt, T1B * B, B, at_core, 2, (txt, RELAY * B))
    f_p2f = copies(txt, T0B * B, txt, T2F * B, B, at_pair, 2, (txt, T0A * B))
    f_p2l = copies(txt, T0A * B, txt, T2L * B, B, at_pair, 2, (txt, RELAY * B))
    f_c3f = copies(txt, T2F * B, txt, T3F * B, B, at_core)
    f_c3l = copies(txt, T2L * B, txt, T3L * B, B, at_core, 2)
    b_7t = copies(sp, YX2 * B, rxh, 0, HALF, at_xm)
    b_7b = copies(sp, YX2 * B + HALF, rxh, HALF, HALF, at_xp)
    b_6t = copies(sp, X2 * B, rxh, 2 * HALF, HALF, at_xm)
    b_6b = copies(sp, X2 * B + HALF, rxh, 3 * HALF, HALF, at_xp)
    b_4 = copies(sp, YXM * B, rx, 0 * B, B, at_xm, 2)
    b_5 = copies(sp, YXP * B, rx, 1 * B, B, at_xp, 2)
    b_1 = copies(sp, XM * B, rx, 2 * B, B, at_xm, 2)
    b_2 = copies(sp, XP * B, rx, 3 * B, B, at_xp, 2)
    b_3 = copies(sp, Y * B, rx, 4 * B, B, at_y, 2)
    b_c3l = copies(sg, G3L * B, rg, G3L * B, B, at_core)
    b_c3f = copies(sg, G3F * B, rg, G3F * B, B, at_core)
    b_c1 = copies(sg, G1A * B, rg, G1A * B, 2 * B, at_core)
    b_p2l = copies(sg, G2L * B, rg, G2L * B, B, at_pair, 2)
    b_p2f = copies(sg, G2F * B, rg, G2F * B, B, at_pair, 2)
    b_zr = copies(sg, GR * B, rg, GR * B, B, at_zm, 2)
    b_zs = copies(sg, GS * B, rg, GS * B, B, at_zm, 2)
    l_c = copies(sl, 0, rl, 0, 8, at_core)
    l_p = copies(sl, 8, rl, 8, 8, at_pair)
    l_zr = copies(sl, 16, rl, 16, 8, at_zm)
    l_zs = copies(sl, 24, rl, 24, 8, at_zm)

    def start(*lists):
        for group in lists:
            for c in group:
                c.start()

    def landed(*lists):
        for group in lists:
            for c in group:
                (c[0] if isinstance(c, list) else c).wait_recv()

    def start_choice(group, which):
        for c in group:
            c[which].start()

    temper = jnp.exp(jnp.full((1, B), log_scale[0], jnp.float32))
    offset = bias[0]

    image_load.wait()
    unit, _ = normalized(images)
    img[pl.ds(OWN * B, B), :] = unit.astype(jnp.bfloat16)
    text_load.wait()
    unit, _ = normalized(texts)
    txt[pl.ds(T0B * B, B), :] = unit.astype(jnp.bfloat16)

    pl.semaphore_wait(barrier, len(partners))

    start(f_y, f_xp, f_xm, f_z1)

    @pl.when(core == 0)
    def _():
        start_choice(f_c1b, 0)

    pg[...] = jnp.zeros_like(pg)
    tgr[...] = jnp.zeros_like(tgr)
    loss[...] = jnp.zeros_like(loss)

    def tile(row, rows, first, blocks, diagonal=False):
        cols = blocks * B
        i = img[pl.ds(row, rows), :]
        t = txt[pl.ds(first * B, cols), :]
        scale = jnp.concatenate([temper] * blocks, axis=1)
        logits = (
            lax.dot_general(i, t, (((1,), (1,)), ((), ())), preferred_element_type=jnp.float32)
            * scale
            + offset
        )
        grown = jnp.exp(logits)
        slope = grown * pl.reciprocal(1.0 + grown, approx=True)
        part = rows
        while part > rows // 8:
            part //= 2
            grown = grown[:part] + grown[part:] + grown[:part] * grown[part:]
        logs = jnp.where(
            grown < 0.0078125,
            grown * (1.0 - grown * (0.5 - grown * (1.0 / 3.0))),
            jnp.log(1.0 + grown),
        )
        column = jnp.sum(logs, axis=0, keepdims=True)
        if diagonal:
            at_row = row + lax.broadcasted_iota(jnp.int32, (rows, cols), 0)
            at_col = first * B + lax.broadcasted_iota(jnp.int32, (rows, cols), 1)
            matched = jnp.logical_and(at_row == at_col, at_col < B)
            slope = slope - jnp.where(matched, 1.0, 0.0)
            column = column - jnp.sum(jnp.where(matched, logits, 0.0), axis=0, keepdims=True)
        for k in range(blocks):
            loss[pl.ds(first + k, 1), :] += column[:, k * B : (k + 1) * B]
        low = slope.astype(jnp.bfloat16)
        pg[pl.ds(row, rows), :] += jnp.dot(low, t, preferred_element_type=jnp.float32)
        tgr[pl.ds(first * B, cols), :] += lax.dot_general(
            low, i, (((0,), (0,)), ((), ())), preferred_element_type=jnp.float32
        )

    def tiles(first_slot, slots, first, blocks, diagonal=False):
        def body(k, carry):
            row = pl.multiple_of((first_slot + 2 * k) * B, 2 * B)
            tile(row, 2 * B, first, blocks, diagonal)
            return carry

        lax.fori_loop(0, slots // 2, body, 0)

    landed(f_y[:1])
    start(f_yxp[:1])
    landed(f_y[1:])
    start(f_yxm[1:], f_yxm[:1], f_yxp[1:])

    @pl.when(y_lo == 0)
    def _():
        start_choice(f_p2f, 0)

    landed(f_z1[:1])
    start(f_z2[:1])

    @pl.when(y_lo == 1)
    def _():
        start_choice(f_p2f[:1], 1)

    landed(f_z1[1:])
    start(f_z2[1:])

    @pl.when(y_lo == 1)
    def _():
        start_choice(f_p2f[1:], 1)

    landed(f_xp, f_xm)
    start(f_x2t, f_x2b, f_c1a)
    tiles(OWN, 4, T0B, 2, diagonal=True)

    @pl.when(y_lo == 0)
    def _():
        start_choice(f_p2l, 0)

    landed(f_z2)

    @pl.when(core == 1)
    def _():
        start_choice(f_c1b, 1)

    @pl.when(y_lo == 1)
    def _():
        start_choice(f_p2l, 1)

    landed(f_p2f)
    start(f_c3f)
    landed(f_yxp[:1])
    start(f_yx2t)
    landed(f_yxm[1:])
    start(f_yx2b)
    landed(f_c1a, f_c3f, f_c1b)
    tiles(OWN, 4, T1A, 4)
    landed(f_yxp[1:], f_yxm[:1])
    tiles(YXM, 2, T0B, 6)
    landed(f_p2l[:1])
    start(f_c3l[:1])
    landed(f_p2l[1:])
    start(f_c3l[1:])
    landed(f_x2t, f_x2b, f_yx2t, f_yx2b)
    tiles(X2, 2, T0B, 6)
    landed(f_c3l)
    tiles(X2, 2, T2L, 2)

    def stage(row, rows):
        sp[pl.ds(row, rows), :] = pg[pl.ds(row, rows), :].astype(jnp.bfloat16)

    def stage_sum(row, half):
        total = pg[pl.ds(row, HALF), :] + rxh[pl.ds(half * HALF, HALF), :].astype(jnp.float32)
        sp[pl.ds(row, HALF), :] = total.astype(jnp.bfloat16)

    def text_sum(slot, k=0, rows=B):
        return tgr[pl.ds(slot * B + k * HALF, rows), :]

    def put(slot, value, k=0):
        sg[pl.ds(slot * B + k * HALF, value.shape[0]), :] = value.astype(jnp.bfloat16)

    def got(slot, k=0, rows=B):
        return rg[pl.ds(slot * B + k * HALF, rows), :].astype(jnp.float32)

    stage(YX2 * B, B)
    start(b_7t, b_7b)
    stage(X2 * B, B)
    start(b_6t, b_6b)
    tiles(OWN, 6, T2L, 2)
    put(G3L, text_sum(T3L))
    start(b_c3l)
    stage(YXM * B + HALF, HALF)
    start(b_4[1:])
    stage(YXP * B, HALF)
    start(b_5[:1])
    put(G3F, text_sum(T3F))
    start(b_c3f)
    sl[pl.ds(0, 8), :] = loss[...]
    start(l_c)

    for k in range(2):
        if k == 0:
            landed(b_c3l)
        put(G2L, text_sum(T2L, k, HALF) + got(G3L, k, HALF), k)
        start(b_p2l[k : k + 1])

    landed(b_7t)
    stage_sum(YXM * B, 0)
    start(b_4[:1])
    landed(b_7b)
    stage_sum(YXP * B + HALF, 1)
    start(b_5[1:])

    put(G1A, text_sum(T1A))
    put(G1B, text_sum(T1B))
    start(b_c1)
    landed(b_c3f)
    put(G2F, text_sum(T2F) + got(G3F))
    landed(l_c)
    loss_2f = loss[pl.ds(T2F, 1), :] + rl[pl.ds(T3F, 1), :]
    loss_2l = loss[pl.ds(T2L, 1), :] + rl[pl.ds(T3L, 1), :]
    sl[pl.ds(8, 8), :] = jnp.concatenate([loss_2f, loss_2l] * 4, axis=0)
    start(l_p)

    stage(XM * B + HALF, HALF)
    start(b_1[1:])
    stage(XP * B, HALF)
    start(b_2[:1])
    landed(b_6t)
    stage_sum(XM * B, 2)
    start(b_1[:1])
    landed(b_6b)
    stage_sum(XP * B + HALF, 3)
    start(b_2[1:])

    odd = core.astype(jnp.float32)
    high = y_lo.astype(jnp.float32)
    for c in b_p2l:
        c.wait_send()
    start(b_p2f)
    landed(b_c1)
    for k in range(2):
        landed(b_p2l[k : k + 1])
        put(GR, got(G1B, k, HALF) * odd + got(G2L, k, HALF) * high, k)
        start(b_zr[k : k + 1])
    landed(l_p)
    sl[pl.ds(16, 8), :] = jnp.broadcast_to(
        rl[pl.ds(T1B, 1), :] * odd + rl[pl.ds(9, 1), :] * high, (8, B)
    )
    start(l_zr)

    landed(b_4, b_5)
    for k in range(2):
        total = (
            pg[pl.ds(Y * B + k * HALF, HALF), :]
            + rx[pl.ds(0 * B + k * HALF, HALF), :].astype(jnp.float32)
            + rx[pl.ds(1 * B + k * HALF, HALF), :].astype(jnp.float32)
        )
        sp[pl.ds(Y * B + k * HALF, HALF), :] = total.astype(jnp.bfloat16)
        start(b_3[k : k + 1])

    for k in range(2):
        landed(b_p2f[k : k + 1], b_zr[k : k + 1])
        from_pair = got(G2F, k, HALF) * high + got(G2L, k, HALF) * (1.0 - high)
        put(GS, text_sum(T0A, k, HALF) + got(G1A, k, HALF) + from_pair + got(GR, k, HALF), k)
        start(b_zs[k : k + 1])
    landed(l_zr)
    sl[pl.ds(24, 8), :] = jnp.broadcast_to(
        loss[pl.ds(T0A, 1), :]
        + rl[pl.ds(T1A, 1), :]
        + rl[pl.ds(8, 1), :] * high
        + rl[pl.ds(9, 1), :] * (1.0 - high)
        + rl[pl.ds(16, 1), :],
        (8, B),
    )
    start(l_zs)

    wide_temper = jnp.concatenate([temper] * (images.shape[1] // B), axis=1)

    landed(b_1, b_2, b_3)
    image_sum = (
        pg[pl.ds(OWN * B, B), :]
        + rx[pl.ds(2 * B, B), :].astype(jnp.float32)
        + rx[pl.ds(3 * B, B), :].astype(jnp.float32)
        + rx[pl.ds(4 * B, B), :].astype(jnp.float32)
    )
    unit, inverse = normalized(images)
    image_grad[...] = chain_back(unit, inverse, wide_temper * image_sum)

    landed(b_zs, l_zs)
    own_sum = (
        text_sum(T0B) + got(G1B) * (1.0 - odd) + got(G2F) * (1.0 - high) + got(GS)
    )
    unit, inverse = normalized(texts)
    text_grad[...] = chain_back(unit, inverse, wide_temper * own_sum)
    text_loss[...] = (
        loss[pl.ds(T0B, 1), :]
        + rl[pl.ds(T1B, 1), :] * (1.0 - odd)
        + rl[pl.ds(8, 1), :] * (1.0 - high)
        + rl[pl.ds(24, 1), :]
    ) * (1.0 / STEPS)
    for c in sent:
        if all(c is not done for done in b_p2l):
            c.wait_send()


SEMS = 80


def on_device(images, texts, log_scale, bias):
    width = images.shape[1]
    images = pltpu.with_memory_space_constraint(images, pltpu.HBM)
    texts = pltpu.with_memory_space_constraint(texts, pltpu.HBM)
    rows = lambda n, dtype: pltpu.VMEM((n, width), dtype)
    vmem = pl.BlockSpec(memory_space=pltpu.VMEM)
    smem = pl.BlockSpec(memory_space=pltpu.SMEM)
    image_grad, text_grad, text_loss = pl.pallas_call(
        kernel,
        out_shape=(
            jax.ShapeDtypeStruct((B, width), jnp.float32),
            jax.ShapeDtypeStruct((B, width), jnp.float32),
            jax.ShapeDtypeStruct((1, B), jnp.float32),
        ),
        in_specs=[pl.BlockSpec(memory_space=pltpu.HBM)] * 2 + [smem, smem],
        out_specs=(vmem, vmem, vmem),
        scratch_shapes=[
            rows(B, jnp.bfloat16),
            rows(B, jnp.bfloat16),
            rows(8 * B, jnp.bfloat16),
            rows(9 * B, jnp.bfloat16),
            rows(8 * B, jnp.float32),
            rows(8 * B, jnp.float32),
            pltpu.VMEM((8, B), jnp.float32),
            rows(8 * B, jnp.bfloat16),
            rows(4 * HALF, jnp.bfloat16),
            rows(5 * B, jnp.bfloat16),
            rows(8 * B, jnp.bfloat16),
            rows(8 * B, jnp.bfloat16),
            pltpu.VMEM((32, B), jnp.float32),
            pltpu.VMEM((32, B), jnp.float32),
            pltpu.SemaphoreType.DMA((2,)),
            pltpu.SemaphoreType.DMA((SEMS,)),
            pltpu.SemaphoreType.DMA((SEMS,)),
        ],
        compiler_params=pltpu.CompilerParams(
            collective_id=0, has_side_effects=True, vmem_limit_bytes=52 << 20
        ),
        name="window",
    )(images, texts, log_scale, bias)
    return image_grad, text_grad, text_loss.reshape(B)


def solution(mesh):
    return jax.shard_map(
        on_device,
        mesh=mesh,
        in_specs=(P(("blk", "member"), None), P(("blk", "member"), None), P(), P()),
        out_specs=(P(("blk", "member"), None), P(("blk", "member"), None), P(("blk", "member"))),
        check_vma=False,
    )
```

```python
import jax
import jax.numpy as jnp
from jax import lax
from jax.experimental import pallas as pl
from jax.experimental.pallas import tpu as pltpu
from jax.sharding import PartitionSpec as P

STEPS = 8
B = 128
HALF = B // 2
MESH = pl.DeviceIdType.MESH

OWN, XM, XP, Y, YXM, YXP, X2, YX2 = range(8)
T0B, T0A, T1A, T1B, T2F, T3F, T2L, T3L, RELAY = range(9)
G1A, G1B, G2F, G2L, G3F, G3L, GZ, GR, GS = range(9)


def normalized(ref):
    wide = ref[...].astype(jnp.float32)
    inverse = lax.rsqrt(jnp.sum(wide * wide, axis=-1, keepdims=True) + 1e-06)
    return wide * inverse, inverse


def chain_back(unit, inverse, upstream):
    return inverse * (upstream - unit * jnp.sum(unit * upstream, axis=-1, keepdims=True))


def kernel(
    images_in, texts_in, log_scale, bias, image_grad, text_grad, text_loss,
    images, texts, img, txt, pg, tgr, loss, sp, rxh, rx, sg, rg, sl, rl, isem, ssem, rsem,
):
    blk, member = lax.axis_index("blk"), lax.axis_index("member")
    n_blk, n_member = lax.axis_size("blk"), lax.axis_size("member")
    core = blk % 2
    y_lo = (blk // 2) % 2
    at_core = (blk + 1 - 2 * core, member)
    at_pair = (blk + 2 - 4 * y_lo, member)
    at_zp = ((blk + 4) % n_blk, member)
    at_zm = ((blk + n_blk - 4) % n_blk, member)
    at_xp = (blk, (member + 2) % n_member)
    at_xm = (blk, (member + n_member - 2) % n_member)
    at_y = (blk, member + 1 - 2 * (member % 2))

    image_load = pltpu.make_async_copy(images_in, images, isem.at[0])
    text_load = pltpu.make_async_copy(texts_in, texts, isem.at[1])
    image_load.start()
    text_load.start()

    barrier = pltpu.get_barrier_semaphore()
    partners = (at_core, at_pair, at_zp, at_zm, at_xp, at_xm, at_y)
    for device in partners:
        pl.semaphore_signal(barrier, inc=1, device_id=device, device_id_type=MESH)

    used = [0]

    def copies(src, src_row, dst, dst_row, rows, device, pieces=1, other=None):
        out = []
        step = rows // pieces
        for k in range(pieces):
            s = used[0]
            used[0] += 1
            made = [
                pltpu.make_async_remote_copy(
                    src_ref=a.at[pl.ds(r + k * step, step)],
                    dst_ref=dst.at[pl.ds(dst_row + k * step, step)],
                    send_sem=ssem.at[s],
                    recv_sem=rsem.at[s],
                    device_id=device,
                    device_id_type=MESH,
                )
                for a, r in [(src, src_row)] + ([other] if other else [])
            ]
            out.append(made if other else made[0])
        return out

    f_xp = copies(img, OWN * B, img, XM * B, B, at_xp, 2)
    f_xm = copies(img, OWN * B, img, XP * B, B, at_xm, 2)
    f_y = copies(img, OWN * B, img, Y * B, B, at_y, 2)
    f_x2t = copies(img, XM * B, img, X2 * B, HALF, at_xp)
    f_x2b = copies(img, XP * B + HALF, img, X2 * B + HALF, HALF, at_xm)
    f_yxp = copies(img, Y * B, img, YXM * B, B, at_xp, 2)
    f_yxm = copies(img, Y * B, img, YXP * B, B, at_xm, 2)
    f_yx2t = copies(img, YXM * B, img, YX2 * B, HALF, at_xp)
    f_yx2b = copies(img, YXP * B + HALF, img, YX2 * B + HALF, HALF, at_xm)
    f_z1 = copies(txt, T0B * B, txt, T0A * B, B, at_zp, 2)
    f_c1a = copies(txt, T0A * B, txt, T1A * B, B, at_core)
    f_z2 = copies(txt, T0A * B, txt, RELAY * B, B, at_zp, 2)
    f_c1b = copies(txt, T0B * B, txt, T1B * B, B, at_core, 1, (txt, RELAY * B))
    f_p2f = copies(txt, T0B * B, txt, T2F * B, B, at_pair, 2, (txt, T0A * B))
    f_p2l = copies(txt, T0A * B, txt, T2L * B, B, at_pair, 2)
    f_zf = copies(txt, T2F * B, txt, T2L * B, B, at_zp, 2)
    f_c3f = copies(txt, T2F * B, txt, T3F * B, B, at_core)
    f_c3l = copies(txt, T2L * B, txt, T3L * B, B, at_core, 2)
    b_7t = copies(sp, YX2 * B, rxh, 0, HALF, at_xm)
    b_7b = copies(sp, YX2 * B + HALF, rxh, HALF, HALF, at_xp)
    b_6t = copies(sp, X2 * B, rxh, 2 * HALF, HALF, at_xm)
    b_6b = copies(sp, X2 * B + HALF, rxh, 3 * HALF, HALF, at_xp)
    b_4 = copies(sp, YXM * B, rx, 0 * B, B, at_xm, 2)
    b_5 = copies(sp, YXP * B, rx, 1 * B, B, at_xp, 2)
    b_1 = copies(sp, XM * B, rx, 2 * B, B, at_xm, 2)
    b_2 = copies(sp, XP * B, rx, 3 * B, B, at_xp, 2)
    b_3 = copies(sp, Y * B, rx, 4 * B, B, at_y, 2)
    b_c3l = copies(sg, G3L * B, rg, G3L * B, B, at_core, 2)
    b_c3f = copies(sg, G3F * B, rg, G3F * B, B, at_core)
    b_c1 = copies(sg, G1A * B, rg, G1A * B, 2 * B, at_core)
    b_zf = copies(sg, G2L * B, rg, GZ * B, B, at_zm, 2)
    b_p2l = copies(sg, G2L * B, rg, G2L * B, B, at_pair, 2)
    b_p2f = copies(sg, G2F * B, rg, G2F * B, B, at_pair, 2)
    b_zr = copies(rg, G1B * B, rg, GR * B, B, at_zm)
    b_zs = copies(sg, GS * B, rg, GS * B, B, at_zm, 2)
    l_c = copies(sl, 0, rl, 0, 8, at_core)
    l_zf = copies(sl, 8, rl, 8, 8, at_zm)
    l_p = copies(sl, 16, rl, 16, 8, at_pair)
    l_zr = copies(rl, 0, rl, 24, 8, at_zm)
    l_zs = copies(sl, 24, rl, 32, 8, at_zm)

    def start(*lists):
        for group in lists:
            for c in group:
                c.start()

    def landed(*lists):
        for group in lists:
            for c in group:
                (c[0] if isinstance(c, list) else c).wait_recv()

    def left(*lists):
        for group in lists:
            for c in group:
                (c[0] if isinstance(c, list) else c).wait_send()

    def start_choice(group, which):
        for c in group:
            c[which].start()

    temper = jnp.exp(jnp.full((1, B), log_scale[0], jnp.float32))
    offset = bias[0]

    image_load.wait()
    unit, _ = normalized(images)
    img[pl.ds(OWN * B, B), :] = unit.astype(jnp.bfloat16)

    pl.semaphore_wait(barrier, len(partners))

    start(f_y, f_xp, f_xm)
    text_load.wait()
    unit, _ = normalized(texts)
    txt[pl.ds(T0B * B, B), :] = unit.astype(jnp.bfloat16)
    start(f_z1)

    @pl.when(core == 0)
    def _():
        start_choice(f_c1b, 0)

    pg[...] = jnp.zeros_like(pg)
    tgr[...] = jnp.zeros_like(tgr)
    loss[...] = jnp.zeros_like(loss)

    def tile(row, rows, first, blocks, diagonal=False):
        cols = blocks * B
        i = img[pl.ds(row, rows), :]
        t = txt[pl.ds(first * B, cols), :]
        scale = jnp.concatenate([temper] * blocks, axis=1)
        logits = (
            lax.dot_general(i, t, (((1,), (1,)), ((), ())), preferred_element_type=jnp.float32)
            * scale
            + offset
        )
        grown = jnp.exp(logits)
        slope = grown * pl.reciprocal(1.0 + grown, approx=True)
        part = rows
        while part > rows // 8:
            part //= 2
            grown = grown[:part] + grown[part:] + grown[:part] * grown[part:]
        logs = jnp.where(
            grown < 0.0078125,
            grown * (1.0 - grown * (0.5 - grown * (1.0 / 3.0))),
            jnp.log(1.0 + grown),
        )
        column = jnp.sum(logs, axis=0, keepdims=True)
        if diagonal:
            at_row = row + lax.broadcasted_iota(jnp.int32, (rows, cols), 0)
            at_col = first * B + lax.broadcasted_iota(jnp.int32, (rows, cols), 1)
            matched = jnp.logical_and(at_row == at_col, at_col < B)
            slope = slope - jnp.where(matched, 1.0, 0.0)
            column = column - jnp.sum(jnp.where(matched, logits, 0.0), axis=0, keepdims=True)
        for k in range(blocks):
            loss[pl.ds(first + k, 1), :] += column[:, k * B : (k + 1) * B]
        low = slope.astype(jnp.bfloat16)
        pg[pl.ds(row, rows), :] += jnp.dot(low, t, preferred_element_type=jnp.float32)
        tgr[pl.ds(first * B, cols), :] += lax.dot_general(
            low, i, (((0,), (0,)), ((), ())), preferred_element_type=jnp.float32
        )

    landed(f_y[:1])
    start(f_yxp[:1])
    landed(f_z1[:1])

    @pl.when(core == 1)
    def _():
        start(f_z2[:1])

    landed(f_y[1:])
    start(f_yxm[1:], f_yxm[:1], f_yxp[1:])

    @pl.when(y_lo == 0)
    def _():
        start_choice(f_p2f, 0)

    @pl.when(y_lo == 1)
    def _():
        start_choice(f_p2f[:1], 1)

    landed(f_z1[1:])

    @pl.when(core == 1)
    def _():
        start(f_z2[1:])

    @pl.when(y_lo == 1)
    def _():
        start_choice(f_p2f[1:], 1)

    start(f_c1a)
    landed(f_xp, f_xm)
    start(f_x2t, f_x2b)
    tile(OWN * B, 4 * B, T0B, 2, diagonal=True)

    @pl.when(y_lo == 0)
    def _():
        start(f_p2l)

    landed(f_yxp[:1])
    start(f_yx2t)
    landed(f_yxm[1:])
    start(f_yx2b)

    @pl.when(y_lo == 0)
    def _():
        landed(f_p2f[:1])
        start(f_zf[:1])

    @pl.when(core == 1)
    def _():
        landed(f_z2)
        start_choice(f_c1b, 1)

    landed(f_c1a, f_c1b)
    tile(OWN * B, 4 * B, T1A, 2)

    @pl.when(y_lo == 0)
    def _():
        landed(f_p2f[1:])
        start(f_zf[1:])

    @pl.when(y_lo == 1)
    def _():
        landed(f_p2f)

    start(f_c3f)
    landed(f_c3f)
    tile(OWN * B, 4 * B, T2F, 2)
    landed(f_yxp[1:], f_yxm[:1])
    tile(YXM * B, 2 * B, T0B, 6)
    for k in range(2):

        @pl.when(y_lo == 0)
        def _():
            landed(f_zf[k : k + 1])

        @pl.when(y_lo == 1)
        def _():
            landed(f_p2l[k : k + 1])

        start(f_c3l[k : k + 1])
    landed(f_c3l)
    tile(YXM * B, 2 * B, T2L, 2)
    landed(f_x2t, f_x2b, f_yx2t, f_yx2b)
    tile(X2 * B, 2 * B, T0B, 8)

    def stage(row, rows):
        sp[pl.ds(row, rows), :] = pg[pl.ds(row, rows), :].astype(jnp.bfloat16)

    def stage_sum(row, half):
        total = pg[pl.ds(row, HALF), :] + rxh[pl.ds(half * HALF, HALF), :].astype(jnp.float32)
        sp[pl.ds(row, HALF), :] = total.astype(jnp.bfloat16)

    def text_sum(slot, k=0, rows=B):
        return tgr[pl.ds(slot * B + k * HALF, rows), :]

    def put(slot, value, k=0):
        sg[pl.ds(slot * B + k * HALF, value.shape[0]), :] = value.astype(jnp.bfloat16)

    def got(slot, k=0, rows=B):
        return rg[pl.ds(slot * B + k * HALF, rows), :].astype(jnp.float32)

    stage(YX2 * B, B)
    start(b_7t, b_7b)
    stage(YXM * B + HALF, HALF)
    start(b_4[1:])
    stage(YXP * B, HALF)
    start(b_5[:1])
    put(G3F, text_sum(T3F))
    start(b_c3f)
    put(G1A, text_sum(T1A))
    put(G1B, text_sum(T1B))
    start(b_c1)
    stage(X2 * B, B)
    start(b_6t, b_6b)
    tile(OWN * B, 4 * B, T2L, 2)
    for k in range(2):
        put(G3L, text_sum(T3L, k, HALF), k)
        start(b_c3l[k : k + 1])
    sl[pl.ds(0, 8), :] = loss[...]
    start(l_c)

    landed(b_7t)
    stage_sum(YXM * B, 0)
    start(b_4[:1])
    landed(b_7b)
    stage_sum(YXP * B + HALF, 1)
    start(b_5[1:])

    for k in range(2):
        landed(b_c3l[k : k + 1])
        put(G2L, text_sum(T2L, k, HALF) + got(G3L, k, HALF), k)

        @pl.when(y_lo == 0)
        def _():
            start(b_zf[k : k + 1])

        @pl.when(y_lo == 1)
        def _():
            start(b_p2l[k : k + 1])

    landed(b_c3f, l_c)
    loss_2f = loss[pl.ds(T2F, 1), :] + rl[pl.ds(T3F, 1), :]
    loss_2l = loss[pl.ds(T2L, 1), :] + rl[pl.ds(T3L, 1), :]

    @pl.when(y_lo == 0)
    def _():
        sl[pl.ds(8, 8), :] = jnp.broadcast_to(loss_2l, (8, B))
        start(l_zf)

    landed(b_c1)

    @pl.when(core == 1)
    def _():
        start(b_zr, l_zr)

    @pl.when(y_lo == 1)
    def _():
        sl[pl.ds(16, 8), :] = jnp.concatenate([loss_2f, loss_2l] * 4, axis=0)
        start(l_p)
        put(G2F, text_sum(T2F) + got(G3F))
        left(b_p2l)
        start(b_p2f)

    stage(XM * B + HALF, HALF)
    start(b_1[1:])
    stage(XP * B, HALF)
    start(b_2[:1])
    landed(b_6t)
    stage_sum(XM * B, 2)
    start(b_1[:1])
    landed(b_6b)
    stage_sum(XP * B + HALF, 3)
    start(b_2[1:])

    @pl.when(y_lo == 0)
    def _():
        for k in range(2):
            landed(b_zf[k : k + 1])
            total = text_sum(T2F, k, HALF) + got(G3F, k, HALF) + got(GZ, k, HALF)
            put(G2F, total, k)
            start(b_p2f[k : k + 1])
        landed(l_zf)
        sl[pl.ds(16, 8), :] = jnp.broadcast_to(loss_2f + rl[pl.ds(8, 1), :], (8, B))
        start(l_p)

    landed(b_4, b_5)
    for k in range(2):
        total = (
            pg[pl.ds(Y * B + k * HALF, HALF), :]
            + rx[pl.ds(0 * B + k * HALF, HALF), :].astype(jnp.float32)
            + rx[pl.ds(1 * B + k * HALF, HALF), :].astype(jnp.float32)
        )
        sp[pl.ds(Y * B + k * HALF, HALF), :] = total.astype(jnp.bfloat16)
        start(b_3[k : k + 1])

    @pl.when(core == 1)
    def _():
        landed(b_zr, l_zr)
        tgr[pl.ds(T0A * B, B), :] += got(GR)
        loss[pl.ds(T0A, 1), :] += rl[pl.ds(24 + T1B, 1), :]

    for k in range(2):

        @pl.when(y_lo == 0)
        def _():
            landed(b_p2l[k : k + 1])
            put(GS, text_sum(T0A, k, HALF) + got(G1A, k, HALF) + got(G2L, k, HALF), k)

        @pl.when(y_lo == 1)
        def _():
            landed(b_p2f[k : k + 1])
            put(GS, text_sum(T0A, k, HALF) + got(G1A, k, HALF) + got(G2F, k, HALF), k)

        start(b_zs[k : k + 1])

    landed(l_p)
    loss_s = loss[pl.ds(T0A, 1), :] + rl[pl.ds(T1A, 1), :]

    @pl.when(y_lo == 0)
    def _():
        sl[pl.ds(24, 8), :] = jnp.broadcast_to(loss_s + rl[pl.ds(17, 1), :], (8, B))
        landed(b_p2f)
        tgr[pl.ds(T0B * B, B), :] += got(G2F)
        loss[pl.ds(T0B, 1), :] += rl[pl.ds(16, 1), :]

    @pl.when(y_lo == 1)
    def _():
        sl[pl.ds(24, 8), :] = jnp.broadcast_to(loss_s + rl[pl.ds(16, 1), :], (8, B))

    start(l_zs)

    @pl.when(core == 0)
    def _():
        tgr[pl.ds(T0B * B, B), :] += got(G1B)
        loss[pl.ds(T0B, 1), :] += rl[pl.ds(T1B, 1), :]

    wide_temper = jnp.concatenate([temper] * (images.shape[1] // B), axis=1)

    landed(b_1, b_2, b_3)
    image_sum = (
        pg[pl.ds(OWN * B, B), :]
        + rx[pl.ds(2 * B, B), :].astype(jnp.float32)
        + rx[pl.ds(3 * B, B), :].astype(jnp.float32)
        + rx[pl.ds(4 * B, B), :].astype(jnp.float32)
    )
    unit, inverse = normalized(images)
    image_grad[...] = chain_back(unit, inverse, wide_temper * image_sum)

    landed(b_zs, l_zs)
    unit, inverse = normalized(texts)
    text_grad[...] = chain_back(unit, inverse, wide_temper * (text_sum(T0B) + got(GS)))
    text_loss[...] = (loss[pl.ds(T0B, 1), :] + rl[pl.ds(32, 1), :]) * (1.0 / STEPS)

    left(f_xp, f_xm, f_y, f_x2t, f_x2b, f_yxp, f_yxm, f_yx2t, f_yx2b)
    left(f_z1, f_c1a, f_c1b, f_p2f, f_c3f, f_c3l)
    left(b_7t, b_7b, b_6t, b_6b, b_4, b_5, b_1, b_2, b_3)
    left(b_c3l, b_c3f, b_c1, b_p2f, b_zs, l_c, l_p, l_zs)

    @pl.when(core == 1)
    def _():
        left(f_z2, b_zr, l_zr)

    @pl.when(y_lo == 0)
    def _():
        left(f_p2l, f_zf, b_zf, l_zf)


SEMS = 80


def on_device(images, texts, log_scale, bias):
    width = images.shape[1]
    images = pltpu.with_memory_space_constraint(images, pltpu.HBM)
    texts = pltpu.with_memory_space_constraint(texts, pltpu.HBM)
    rows = lambda n, dtype: pltpu.VMEM((n, width), dtype)
    vmem = pl.BlockSpec(memory_space=pltpu.VMEM)
    smem = pl.BlockSpec(memory_space=pltpu.SMEM)
    image_grad, text_grad, text_loss = pl.pallas_call(
        kernel,
        out_shape=(
            jax.ShapeDtypeStruct((B, width), jnp.float32),
            jax.ShapeDtypeStruct((B, width), jnp.float32),
            jax.ShapeDtypeStruct((1, B), jnp.float32),
        ),
        in_specs=[pl.BlockSpec(memory_space=pltpu.HBM)] * 2 + [smem, smem],
        out_specs=(vmem, vmem, vmem),
        scratch_shapes=[
            rows(B, jnp.bfloat16),
            rows(B, jnp.bfloat16),
            rows(8 * B, jnp.bfloat16),
            rows(9 * B, jnp.bfloat16),
            rows(8 * B, jnp.float32),
            rows(8 * B, jnp.float32),
            pltpu.VMEM((8, B), jnp.float32),
            rows(8 * B, jnp.bfloat16),
            rows(4 * HALF, jnp.bfloat16),
            rows(5 * B, jnp.bfloat16),
            rows(9 * B, jnp.bfloat16),
            rows(9 * B, jnp.bfloat16),
            pltpu.VMEM((32, B), jnp.float32),
            pltpu.VMEM((40, B), jnp.float32),
            pltpu.SemaphoreType.DMA((2,)),
            pltpu.SemaphoreType.DMA((SEMS,)),
            pltpu.SemaphoreType.DMA((SEMS,)),
        ],
        compiler_params=pltpu.CompilerParams(
            collective_id=0, has_side_effects=True, vmem_limit_bytes=52 << 20
        ),
        name="window",
    )(images, texts, log_scale, bias)
    return image_grad, text_grad, text_loss.reshape(B)


def solution(mesh):
    return jax.shard_map(
        on_device,
        mesh=mesh,
        in_specs=(P(("blk", "member"), None), P(("blk", "member"), None), P(), P()),
        out_specs=(P(("blk", "member"), None), P(("blk", "member"), None), P(("blk", "member"))),
        check_vma=False,
    )
```

```python
import jax
import jax.numpy as jnp
from jax import lax
from jax.experimental import pallas as pl
from jax.experimental.pallas import tpu as pltpu
from jax.sharding import PartitionSpec as P

STEPS = 8
B = 128
HALF = B // 2
MESH = pl.DeviceIdType.MESH

OWN, XM, XP, Y, YXM, YXP, X2, YX2 = range(8)
T0B, T0A, T1A, T1B, T2F, T3F, T2L, T3L, RELAY = range(9)
G1A, G1B, G2F, G2L, G3F, G3L, GR, GS = range(8)


def normalized(ref):
    wide = ref[...].astype(jnp.float32)
    inverse = lax.rsqrt(jnp.sum(wide * wide, axis=-1, keepdims=True) + 1e-06)
    return wide * inverse, inverse


def chain_back(unit, inverse, upstream):
    return inverse * (upstream - unit * jnp.sum(unit * upstream, axis=-1, keepdims=True))


def kernel(
    images_in, texts_in, log_scale, bias, image_grad, text_grad, text_loss,
    images, texts, img, txt, pg, tgr, loss, sp, rxh, rx, sg, rg, sl, rl, isem, ssem, rsem,
):
    blk, member = lax.axis_index("blk"), lax.axis_index("member")
    n_blk, n_member = lax.axis_size("blk"), lax.axis_size("member")
    core = blk % 2
    y_lo = (blk // 2) % 2
    z = blk // 4
    at_core = (blk + 1 - 2 * core, member)
    at_pair = (blk + 2 - 4 * y_lo, member)
    at_zp = ((blk + 4) % n_blk, member)
    at_zm = ((blk + n_blk - 4) % n_blk, member)
    at_xp = (blk, (member + 2) % n_member)
    at_xm = (blk, (member + n_member - 2) % n_member)
    at_y = (blk, member + 1 - 2 * (member % 2))

    image_load = pltpu.make_async_copy(images_in, images, isem.at[0])
    text_load = pltpu.make_async_copy(texts_in, texts, isem.at[1])
    image_load.start()
    text_load.start()

    barrier = pltpu.get_barrier_semaphore()
    partners = (at_core, at_pair, at_zm, at_xp, at_xm, at_y)
    for device in partners:
        pl.semaphore_signal(barrier, inc=1, device_id=device, device_id_type=MESH)

    used = [0]

    def copies(src, src_row, dst, dst_row, rows, device, pieces=1, other=None):
        out = []
        step = rows // pieces
        for k in range(pieces):
            s = used[0]
            used[0] += 1
            made = [
                pltpu.make_async_remote_copy(
                    src_ref=a.at[pl.ds(r + k * step, step)],
                    dst_ref=dst.at[pl.ds(dst_row + k * step, step)],
                    send_sem=ssem.at[s],
                    recv_sem=rsem.at[s],
                    device_id=device,
                    device_id_type=MESH,
                )
                for a, r in [(src, src_row)] + ([other] if other else [])
            ]
            out.append(made if other else made[0])
        return out

    f_xp = copies(img, OWN * B, img, XM * B, B, at_xp, 2)
    f_xm = copies(img, OWN * B, img, XP * B, B, at_xm, 2)
    f_y = copies(img, OWN * B, img, Y * B, B, at_y, 2)
    f_x2t = copies(img, XM * B, img, X2 * B, HALF, at_xp)
    f_x2b = copies(img, XP * B + HALF, img, X2 * B + HALF, HALF, at_xm)
    f_yxp = copies(img, Y * B, img, YXM * B, B, at_xp, 2)
    f_yxm = copies(img, Y * B, img, YXP * B, B, at_xm, 2)
    f_yx2t = copies(img, YXM * B, img, YX2 * B, HALF, at_xp)
    f_yx2b = copies(img, YXP * B + HALF, img, YX2 * B + HALF, HALF, at_xm)
    f_z1 = copies(txt, T0B * B, txt, T0A * B, B, at_zp, 2)
    f_c1a = copies(txt, T0A * B, txt, T1A * B, B, at_core)
    f_z2 = copies(txt, T0A * B, txt, RELAY * B, B, at_zp, 2)
    f_c1b = copies(txt, T0B * B, txt, T1B * B, B, at_core, 1, (txt, RELAY * B))
    f_p2f = copies(txt, T0B * B, txt, T2F * B, B, at_pair, 2, (txt, T0A * B))
    f_p2l = copies(txt, T0A * B, txt, T2L * B, B, at_pair, 2)
    f_zf = copies(txt, T2F * B, txt, T2L * B, B, at_zp, 2)
    f_c3f = copies(txt, T2F * B, txt, T3F * B, B, at_core)
    f_c3l = copies(txt, T2L * B, txt, T3L * B, B, at_core, 2)
    b_7t = copies(sp, YX2 * B, rxh, 0, HALF, at_xm)
    b_7b = copies(sp, YX2 * B + HALF, rxh, HALF, HALF, at_xp)
    b_6t = copies(sp, X2 * B, rxh, 2 * HALF, HALF, at_xm)
    b_6b = copies(sp, X2 * B + HALF, rxh, 3 * HALF, HALF, at_xp)
    b_4 = copies(sp, YXM * B, rx, 0 * B, B, at_xm, 2)
    b_5 = copies(sp, YXP * B, rx, 1 * B, B, at_xp, 2)
    b_1 = copies(sp, XM * B, rx, 2 * B, B, at_xm, 2)
    b_2 = copies(sp, XP * B, rx, 3 * B, B, at_xp, 2)
    b_3 = copies(sp, Y * B, rx, 4 * B, B, at_y, 2)
    b_c3l = copies(sg, G3L * B, rg, G3L * B, B, at_core, 2)
    b_c3f = copies(sg, G3F * B, rg, G3F * B, B, at_core)
    b_c1 = copies(sg, G1A * B, rg, G1A * B, 2 * B, at_core)
    b_p2l = copies(sg, G2L * B, rg, G2L * B, B, at_pair, 2)
    b_p2f = copies(sg, G2F * B, rg, G2F * B, B, at_pair, 2)
    b_zr = copies(sg, GR * B, rg, GR * B, B, at_zm, 2)
    b_zs = copies(sg, GS * B, rg, GS * B, B, at_zm, 2)
    l_c = copies(sl, 0, rl, 0, 8, at_core)
    l_p = copies(sl, 8, rl, 8, 8, at_pair)
    l_zr = copies(sl, 16, rl, 16, 8, at_zm)
    l_zs = copies(sl, 24, rl, 24, 8, at_zm)

    def start(*lists):
        for group in lists:
            for c in group:
                c.start()

    def landed(*lists):
        for group in lists:
            for c in group:
                (c[0] if isinstance(c, list) else c).wait_recv()

    def left(*lists):
        for group in lists:
            for c in group:
                (c[0] if isinstance(c, list) else c).wait_send()

    def start_choice(group, which):
        for c in group:
            c[which].start()

    temper = jnp.exp(jnp.full((1, B), log_scale[0], jnp.float32))
    offset = bias[0]

    text_load.wait()
    unit, _ = normalized(texts)
    txt[pl.ds(T0B * B, B), :] = unit.astype(jnp.bfloat16)

    pl.semaphore_wait(barrier, len(partners))

    start(f_z1)
    image_load.wait()
    unit, _ = normalized(images)
    img[pl.ds(OWN * B, B), :] = unit.astype(jnp.bfloat16)
    start(f_y, f_xp, f_xm)

    @pl.when(core == 0)
    def _():
        start_choice(f_c1b, 0)

    pg[...] = jnp.zeros_like(pg)
    tgr[...] = jnp.zeros_like(tgr)
    loss[...] = jnp.zeros_like(loss)

    def tile(row, rows, first, blocks, diagonal=False):
        cols = blocks * B
        i = img[pl.ds(row, rows), :]
        t = txt[pl.ds(first * B, cols), :]
        scale = jnp.concatenate([temper] * blocks, axis=1)
        logits = (
            lax.dot_general(i, t, (((1,), (1,)), ((), ())), preferred_element_type=jnp.float32)
            * scale
            + offset
        )
        grown = jnp.exp(logits)
        slope = grown * pl.reciprocal(1.0 + grown, approx=True)
        part = rows
        while part > rows // 8:
            part //= 2
            grown = grown[:part] + grown[part:] + grown[:part] * grown[part:]
        logs = jnp.where(
            grown < 0.0078125,
            grown * (1.0 - grown * (0.5 - grown * (1.0 / 3.0))),
            jnp.log(1.0 + grown),
        )
        column = jnp.sum(logs, axis=0, keepdims=True)
        if diagonal:
            at_row = row + lax.broadcasted_iota(jnp.int32, (rows, cols), 0)
            at_col = first * B + lax.broadcasted_iota(jnp.int32, (rows, cols), 1)
            matched = jnp.logical_and(at_row == at_col, at_col < B)
            slope = slope - jnp.where(matched, 1.0, 0.0)
            column = column - jnp.sum(jnp.where(matched, logits, 0.0), axis=0, keepdims=True)
        for k in range(blocks):
            loss[pl.ds(first + k, 1), :] += column[:, k * B : (k + 1) * B]
        low = slope.astype(jnp.bfloat16)
        pg[pl.ds(row, rows), :] += jnp.dot(low, t, preferred_element_type=jnp.float32)
        tgr[pl.ds(first * B, cols), :] += lax.dot_general(
            low, i, (((0,), (0,)), ((), ())), preferred_element_type=jnp.float32
        )

    def from_z(k):
        landed(f_z1[k : k + 1])

        @pl.when(core == 1)
        def _():
            start(f_z2[k : k + 1])

        @pl.when(y_lo == 1)
        def _():
            start_choice(f_p2f[k : k + 1], 1)

    def from_y(k):
        landed(f_y[k : k + 1])
        if k == 0:
            start(f_yxp[:1])
        else:
            start(f_yxm[1:], f_yxm[:1], f_yxp[1:])

            @pl.when(y_lo == 0)
            def _():
                start_choice(f_p2f, 0)

    def round_x():
        landed(f_xp, f_xm)
        start(f_x2t, f_x2b)

    def round_yx():
        landed(f_yxp[:1])
        start(f_yx2t)
        landed(f_yxm[1:])
        start(f_yx2b)

    @pl.when(z == 0)
    def _():
        from_y(0)
        from_y(1)
        round_x()
        round_yx()
        from_z(0)
        from_z(1)

    @pl.when(z > 0)
    def _():
        from_z(0)
        from_y(0)
        from_z(1)
        from_y(1)
        round_x()

    start(f_c1a)
    tile(OWN * B, 4 * B, T0B, 2, diagonal=True)

    @pl.when(z > 0)
    def _():
        round_yx()

    @pl.when(y_lo == 0)
    def _():
        start(f_p2l)
        landed(f_p2f[:1])
        start(f_zf[:1])
        landed(f_p2f[1:])
        start(f_zf[1:])

    @pl.when(core == 1)
    def _():
        landed(f_z2)
        start_choice(f_c1b, 1)

    landed(f_c1a, f_c1b)
    tile(OWN * B, 4 * B, T1A, 2)

    @pl.when(y_lo == 1)
    def _():
        landed(f_p2f)

    start(f_c3f)
    landed(f_yxp[1:], f_yxm[:1], f_c3f)
    tile(OWN * B, 4 * B, T2F, 2)
    tile(YXM * B, 2 * B, T0B, 6)
    landed(f_x2t, f_x2b, f_yx2t, f_yx2b)
    tile(X2 * B, 2 * B, T0B, 6)

    def stage(row, rows):
        sp[pl.ds(row, rows), :] = pg[pl.ds(row, rows), :].astype(jnp.bfloat16)

    def stage_sum(row, half):
        total = pg[pl.ds(row, HALF), :] + rxh[pl.ds(half * HALF, HALF), :].astype(jnp.float32)
        sp[pl.ds(row, HALF), :] = total.astype(jnp.bfloat16)

    def text_sum(slot, k=0, rows=B):
        return tgr[pl.ds(slot * B + k * HALF, rows), :]

    def put(slot, value, k=0):
        sg[pl.ds(slot * B + k * HALF, value.shape[0]), :] = value.astype(jnp.bfloat16)

    def got(slot, k=0, rows=B):
        return rg[pl.ds(slot * B + k * HALF, rows), :].astype(jnp.float32)

    for k in range(2):

        @pl.when(y_lo == 0)
        def _():
            landed(f_zf[k : k + 1])

        @pl.when(y_lo == 1)
        def _():
            landed(f_p2l[k : k + 1])

        start(f_c3l[k : k + 1])
    put(G3F, text_sum(T3F))
    start(b_c3f)
    put(G1A, text_sum(T1A))
    put(G1B, text_sum(T1B))
    start(b_c1)
    landed(f_c3l)
    tile(X2 * B, 2 * B, T2L, 2)
    stage(YX2 * B, B)
    start(b_7t, b_7b)
    stage(X2 * B, B)
    start(b_6t, b_6b)
    tile(YXM * B, 2 * B, T2L, 2)
    stage(YXM * B + HALF, HALF)
    start(b_4[1:])
    stage(YXP * B, HALF)
    start(b_5[:1])
    tile(OWN * B, 4 * B, T2L, 2)
    for k in range(2):
        put(G3L, text_sum(T3L, k, HALF), k)
        start(b_c3l[k : k + 1])
    sl[pl.ds(0, 8), :] = loss[...]
    start(l_c)

    landed(b_7t)
    stage_sum(YXM * B, 0)
    start(b_4[:1])
    landed(b_7b)
    stage_sum(YXP * B + HALF, 1)
    start(b_5[1:])

    for k in range(2):
        landed(b_c3l[k : k + 1])
        put(G2L, text_sum(T2L, k, HALF) + got(G3L, k, HALF), k)
        start(b_p2l[k : k + 1])

    stage(XM * B + HALF, HALF)
    start(b_1[1:])
    stage(XP * B, HALF)
    start(b_2[:1])
    landed(b_6t)
    stage_sum(XM * B, 2)
    start(b_1[:1])
    landed(b_6b)
    stage_sum(XP * B + HALF, 3)
    start(b_2[1:])

    landed(b_c3f)
    put(G2F, text_sum(T2F) + got(G3F))
    landed(l_c)
    loss_2f = loss[pl.ds(T2F, 1), :] + rl[pl.ds(T3F, 1), :]
    loss_2l = loss[pl.ds(T2L, 1), :] + rl[pl.ds(T3L, 1), :]
    sl[pl.ds(8, 8), :] = jnp.concatenate([loss_2f, loss_2l] * 4, axis=0)
    start(l_p)
    left(b_p2l)
    start(b_p2f)

    odd = core.astype(jnp.float32)
    high = y_lo.astype(jnp.float32)
    landed(b_c1)
    for k in range(2):
        landed(b_p2l[k : k + 1])
        put(GR, got(G1B, k, HALF) * odd + got(G2L, k, HALF) * high, k)
        start(b_zr[k : k + 1])
    landed(l_p)
    sl[pl.ds(16, 8), :] = jnp.broadcast_to(
        rl[pl.ds(T1B, 1), :] * odd + rl[pl.ds(9, 1), :] * high, (8, B)
    )
    start(l_zr)

    landed(b_4, b_5)
    for k in range(2):
        total = (
            pg[pl.ds(Y * B + k * HALF, HALF), :]
            + rx[pl.ds(0 * B + k * HALF, HALF), :].astype(jnp.float32)
            + rx[pl.ds(1 * B + k * HALF, HALF), :].astype(jnp.float32)
        )
        sp[pl.ds(Y * B + k * HALF, HALF), :] = total.astype(jnp.bfloat16)
        start(b_3[k : k + 1])

    for k in range(2):
        landed(b_p2f[k : k + 1], b_zr[k : k + 1])
        from_pair = got(G2F, k, HALF) * high + got(G2L, k, HALF) * (1.0 - high)
        put(GS, text_sum(T0A, k, HALF) + got(G1A, k, HALF) + from_pair + got(GR, k, HALF), k)
        start(b_zs[k : k + 1])
    landed(l_zr)
    sl[pl.ds(24, 8), :] = jnp.broadcast_to(
        loss[pl.ds(T0A, 1), :]
        + rl[pl.ds(T1A, 1), :]
        + rl[pl.ds(8, 1), :] * high
        + rl[pl.ds(9, 1), :] * (1.0 - high)
        + rl[pl.ds(16, 1), :],
        (8, B),
    )
    start(l_zs)

    wide_temper = jnp.concatenate([temper] * (images.shape[1] // B), axis=1)

    landed(b_1, b_2, b_3)
    image_sum = (
        pg[pl.ds(OWN * B, B), :]
        + rx[pl.ds(2 * B, B), :].astype(jnp.float32)
        + rx[pl.ds(3 * B, B), :].astype(jnp.float32)
        + rx[pl.ds(4 * B, B), :].astype(jnp.float32)
    )
    unit, inverse = normalized(images)
    image_grad[...] = chain_back(unit, inverse, wide_temper * image_sum)

    landed(b_zs, l_zs)
    own_sum = (
        text_sum(T0B) + got(G1B) * (1.0 - odd) + got(G2F) * (1.0 - high) + got(GS)
    )
    unit, inverse = normalized(texts)
    text_grad[...] = chain_back(unit, inverse, wide_temper * own_sum)
    text_loss[...] = (
        loss[pl.ds(T0B, 1), :]
        + rl[pl.ds(T1B, 1), :] * (1.0 - odd)
        + rl[pl.ds(8, 1), :] * (1.0 - high)
        + rl[pl.ds(24, 1), :]
    ) * (1.0 / STEPS)

    left(f_xp, f_xm, f_y, f_x2t, f_x2b, f_yxp, f_yxm, f_yx2t, f_yx2b)
    left(f_z1, f_c1a, f_c1b, f_p2f, f_c3f, f_c3l)
    left(b_7t, b_7b, b_6t, b_6b, b_4, b_5, b_1, b_2, b_3)
    left(b_c3l, b_c3f, b_c1, b_p2f, b_zr, b_zs, l_c, l_p, l_zr, l_zs)

    @pl.when(core == 1)
    def _():
        left(f_z2)

    @pl.when(y_lo == 0)
    def _():
        left(f_p2l, f_zf)


SEMS = 80


def on_device(images, texts, log_scale, bias):
    width = images.shape[1]
    images = pltpu.with_memory_space_constraint(images, pltpu.HBM)
    texts = pltpu.with_memory_space_constraint(texts, pltpu.HBM)
    rows = lambda n, dtype: pltpu.VMEM((n, width), dtype)
    vmem = pl.BlockSpec(memory_space=pltpu.VMEM)
    smem = pl.BlockSpec(memory_space=pltpu.SMEM)
    image_grad, text_grad, text_loss = pl.pallas_call(
        kernel,
        out_shape=(
            jax.ShapeDtypeStruct((B, width), jnp.float32),
            jax.ShapeDtypeStruct((B, width), jnp.float32),
            jax.ShapeDtypeStruct((1, B), jnp.float32),
        ),
        in_specs=[pl.BlockSpec(memory_space=pltpu.HBM)] * 2 + [smem, smem],
        out_specs=(vmem, vmem, vmem),
        scratch_shapes=[
            rows(B, jnp.bfloat16),
            rows(B, jnp.bfloat16),
            rows(8 * B, jnp.bfloat16),
            rows(9 * B, jnp.bfloat16),
            rows(8 * B, jnp.float32),
            rows(8 * B, jnp.float32),
            pltpu.VMEM((8, B), jnp.float32),
            rows(8 * B, jnp.bfloat16),
            rows(4 * HALF, jnp.bfloat16),
            rows(5 * B, jnp.bfloat16),
            rows(8 * B, jnp.bfloat16),
            rows(8 * B, jnp.bfloat16),
            pltpu.VMEM((32, B), jnp.float32),
            pltpu.VMEM((32, B), jnp.float32),
            pltpu.SemaphoreType.DMA((2,)),
            pltpu.SemaphoreType.DMA((SEMS,)),
            pltpu.SemaphoreType.DMA((SEMS,)),
        ],
        compiler_params=pltpu.CompilerParams(
            collective_id=0, has_side_effects=True, vmem_limit_bytes=52 << 20
        ),
        name="window",
    )(images, texts, log_scale, bias)
    return image_grad, text_grad, text_loss.reshape(B)


def solution(mesh):
    return jax.shard_map(
        on_device,
        mesh=mesh,
        in_specs=(P(("blk", "member"), None), P(("blk", "member"), None), P(), P()),
        out_specs=(P(("blk", "member"), None), P(("blk", "member"), None), P(("blk", "member"))),
        check_vma=False,
    )
```

```python
import jax
import jax.numpy as jnp
from jax import lax
from jax.experimental import pallas as pl
from jax.experimental.pallas import tpu as pltpu
from jax.sharding import PartitionSpec as P

STEPS = 8
B = 128
HALF = B // 2
QUARTER = B // 4
MESH = pl.DeviceIdType.MESH

OWN, XM, XP, Y, YXM, YXP, X2, YX2 = range(8)
T0B, T0A, T1A, T1B, T2F, T3F, T2L, T3L, RELAY = range(9)
G1A, G1B, G2F, G2L, G3F, G3L, GR, GS = range(8)


def normalized(ref):
    wide = ref[...].astype(jnp.float32)
    inverse = lax.rsqrt(jnp.sum(wide * wide, axis=-1, keepdims=True) + 1e-06)
    return wide * inverse, inverse


def chain_back(unit, inverse, upstream):
    return inverse * (upstream - unit * jnp.sum(unit * upstream, axis=-1, keepdims=True))


def kernel(
    images_in, texts_in, log_scale, bias, image_grad, text_grad, text_loss,
    images, texts, img, txt, pg, tgr, loss, sp, rxh, rx, sg, rg, sl, rl, isem, ssem, rsem,
):
    blk, member = lax.axis_index("blk"), lax.axis_index("member")
    n_blk, n_member = lax.axis_size("blk"), lax.axis_size("member")
    core = blk % 2
    y_lo = (blk // 2) % 2
    z = blk // 4
    at_core = (blk + 1 - 2 * core, member)
    at_pair = (blk + 2 - 4 * y_lo, member)
    at_zp = ((blk + 4) % n_blk, member)
    at_zm = ((blk + n_blk - 4) % n_blk, member)
    at_xp = (blk, (member + 2) % n_member)
    at_xm = (blk, (member + n_member - 2) % n_member)
    at_y = (blk, member + 1 - 2 * (member % 2))

    image_load = pltpu.make_async_copy(images_in, images, isem.at[0])
    text_load = pltpu.make_async_copy(texts_in, texts, isem.at[1])
    image_load.start()
    text_load.start()

    barrier = pltpu.get_barrier_semaphore()
    partners = (at_core, at_pair, at_zm, at_xp, at_xm, at_y)
    for device in partners:
        pl.semaphore_signal(barrier, inc=1, device_id=device, device_id_type=MESH)

    used = [0]

    def copies(src, src_row, dst, dst_row, rows, device, pieces=1, other=None):
        out = []
        step = rows // pieces
        for k in range(pieces):
            s = used[0]
            used[0] += 1
            made = [
                pltpu.make_async_remote_copy(
                    src_ref=a.at[pl.ds(r + k * step, step)],
                    dst_ref=dst.at[pl.ds(dst_row + k * step, step)],
                    send_sem=ssem.at[s],
                    recv_sem=rsem.at[s],
                    device_id=device,
                    device_id_type=MESH,
                )
                for a, r in [(src, src_row)] + ([other] if other else [])
            ]
            out.append(made if other else made[0])
        return out

    f_xp = copies(img, OWN * B, img, XM * B, B, at_xp, 2)
    f_xm = copies(img, OWN * B, img, XP * B, B, at_xm, 2)
    f_y = copies(img, OWN * B, img, Y * B, B, at_y, 2)
    f_x2t = copies(img, XM * B, img, X2 * B, HALF, at_xp)
    f_x2b = copies(img, XP * B + HALF, img, X2 * B + HALF, HALF, at_xm)
    f_yxp = copies(img, Y * B, img, YXM * B, B, at_xp, 2)
    f_yxm = copies(img, Y * B, img, YXP * B, B, at_xm, 2)
    f_yx2t = copies(img, YXM * B, img, YX2 * B, QUARTER, at_xp)
    f_yx2b = copies(img, YXP * B + 3 * QUARTER, img, YX2 * B + 3 * QUARTER, QUARTER, at_xm)
    f_yx2y = copies(img, X2 * B + QUARTER, img, YX2 * B + QUARTER, HALF, at_y)
    f_z1 = copies(txt, T0B * B, txt, T0A * B, B, at_zp, 2)
    f_c1a = copies(txt, T0A * B, txt, T1A * B, B, at_core)
    f_z2 = copies(txt, T0A * B, txt, RELAY * B, B, at_zp, 2)
    f_c1b = copies(txt, T0B * B, txt, T1B * B, B, at_core, 1, (txt, RELAY * B))
    f_p2f = copies(txt, T0B * B, txt, T2F * B, B, at_pair, 2, (txt, T0A * B))
    f_p2l = copies(txt, T0A * B, txt, T2L * B, B, at_pair, 2)
    f_zf = copies(txt, T2F * B, txt, T2L * B, B, at_zp, 2)
    f_c3f = copies(txt, T2F * B, txt, T3F * B, B, at_core)
    f_c3l = copies(txt, T2L * B, txt, T3L * B, B, at_core, 2)
    b_7t = copies(sp, YX2 * B, rxh, 0, QUARTER, at_xm)
    b_7y = copies(sp, YX2 * B + QUARTER, rxh, QUARTER, HALF, at_y)
    b_7b = copies(sp, YX2 * B + 3 * QUARTER, rxh, 3 * QUARTER, QUARTER, at_xp)
    b_6t = copies(sp, X2 * B, rxh, B, HALF, at_xm)
    b_6b = copies(sp, X2 * B + HALF, rxh, B + HALF, HALF, at_xp)
    b_4s = copies(sp, YXM * B, rx, 0, QUARTER, at_xm)
    b_4 = copies(sp, YXM * B + QUARTER, rx, QUARTER, 3 * QUARTER, at_xm)
    b_5 = copies(sp, YXP * B, rx, B, 3 * QUARTER, at_xp)
    b_5s = copies(sp, YXP * B + 3 * QUARTER, rx, B + 3 * QUARTER, QUARTER, at_xp)
    b_1 = copies(sp, XM * B, rx, 2 * B, B, at_xm, 2)
    b_2 = copies(sp, XP * B, rx, 3 * B, B, at_xp, 2)
    b_3 = copies(sp, Y * B, rx, 4 * B, B, at_y, 2)
    b_c3l = copies(sg, G3L * B, rg, G3L * B, B, at_core, 2)
    b_c3f = copies(sg, G3F * B, rg, G3F * B, B, at_core)
    b_c1 = copies(sg, G1A * B, rg, G1A * B, 2 * B, at_core)
    b_zf = copies(sg, G2L * B, rg, G2L * B, B, at_zm, 2)
    b_p2f = copies(sg, G2F * B, rg, G2F * B, B, at_pair, 2)
    b_zr = copies(rg, G1B * B, rg, GR * B, B, at_zm, 2)
    b_zs = copies(sg, GS * B, rg, GS * B, B, at_zm, 2)
    l_c = copies(sl, 0, rl, 0, 8, at_core)
    l_zf = copies(sl, 8, rl, 8, 8, at_zm)
    l_p = copies(sl, 16, rl, 16, 8, at_pair)
    l_zr = copies(rl, 0, rl, 24, 8, at_zm)
    l_zs = copies(sl, 24, rl, 32, 8, at_zm)

    def start(*lists):
        for group in lists:
            for c in group:
                c.start()

    def landed(*lists):
        for group in lists:
            for c in group:
                (c[0] if isinstance(c, list) else c).wait_recv()

    def left(*lists):
        for group in lists:
            for c in group:
                (c[0] if isinstance(c, list) else c).wait_send()

    def start_choice(group, which):
        for c in group:
            c[which].start()

    temper = jnp.exp(jnp.full((1, B), log_scale[0], jnp.float32))
    offset = bias[0]

    text_load.wait()
    unit, _ = normalized(texts)
    txt[pl.ds(T0B * B, B), :] = unit.astype(jnp.bfloat16)

    pl.semaphore_wait(barrier, len(partners))

    start(f_z1)
    image_load.wait()
    unit, _ = normalized(images)
    img[pl.ds(OWN * B, B), :] = unit.astype(jnp.bfloat16)
    start(f_y, f_xp, f_xm)

    @pl.when(core == 0)
    def _():
        start_choice(f_c1b, 0)

    pg[...] = jnp.zeros_like(pg)
    tgr[...] = jnp.zeros_like(tgr)
    loss[...] = jnp.zeros_like(loss)

    def tile(row, rows, first, blocks, diagonal=False):
        cols = blocks * B
        i = img[pl.ds(row, rows), :]
        t = txt[pl.ds(first * B, cols), :]
        scale = jnp.concatenate([temper] * blocks, axis=1)
        logits = (
            lax.dot_general(i, t, (((1,), (1,)), ((), ())), preferred_element_type=jnp.float32)
            * scale
            + offset
        )
        grown = jnp.exp(logits)
        slope = grown * pl.reciprocal(1.0 + grown, approx=True)
        part = rows
        while part > rows // 8:
            part //= 2
            grown = grown[:part] + grown[part:] + grown[:part] * grown[part:]
        logs = jnp.where(
            grown < 0.0078125,
            grown * (1.0 - grown * (0.5 - grown * (1.0 / 3.0))),
            jnp.log(1.0 + grown),
        )
        column = jnp.sum(logs, axis=0, keepdims=True)
        if diagonal:
            at_row = row + lax.broadcasted_iota(jnp.int32, (rows, cols), 0)
            at_col = first * B + lax.broadcasted_iota(jnp.int32, (rows, cols), 1)
            matched = jnp.logical_and(at_row == at_col, at_col < B)
            slope = slope - jnp.where(matched, 1.0, 0.0)
            column = column - jnp.sum(jnp.where(matched, logits, 0.0), axis=0, keepdims=True)
        for k in range(blocks):
            loss[pl.ds(first + k, 1), :] += column[:, k * B : (k + 1) * B]
        low = slope.astype(jnp.bfloat16)
        pg[pl.ds(row, rows), :] += jnp.dot(low, t, preferred_element_type=jnp.float32)
        tgr[pl.ds(first * B, cols), :] += lax.dot_general(
            low, i, (((0,), (0,)), ((), ())), preferred_element_type=jnp.float32
        )

    def from_z(k):
        landed(f_z1[k : k + 1])

        @pl.when(core == 1)
        def _():
            start(f_z2[k : k + 1])

        @pl.when(y_lo == 1)
        def _():
            start_choice(f_p2f[k : k + 1], 1)

    def from_y(k):
        landed(f_y[k : k + 1])
        if k == 0:
            start(f_yxp[:1])
        else:
            start(f_yxm[1:])

            @pl.when(y_lo == 0)
            def _():
                start_choice(f_p2f, 0)

    def round_x():
        landed(f_xp, f_xm)
        start(f_x2t, f_x2b, f_yxm[:1], f_yxp[1:])

    def round_yx():
        landed(f_yxp[:1])
        start(f_yx2t)
        landed(f_yxm[1:])
        start(f_yx2b)

    @pl.when(z == 0)
    def _():
        from_y(0)
        from_y(1)
        round_x()
        round_yx()
        for k in range(2):
            from_z(k)

            @pl.when(y_lo == 0)
            def _():
                start(f_p2l[k : k + 1])

    @pl.when(z > 0)
    def _():
        from_z(0)
        from_y(0)
        from_z(1)
        from_y(1)
        round_x()

    start(f_c1a)
    tile(OWN * B, 4 * B, T0B, 2, diagonal=True)

    up_z = jnp.logical_or(y_lo == 0, z < n_blk // 4 - 1)
    from_below = jnp.logical_or(y_lo == 0, z > 0)

    def forward(k):
        landed(f_p2f[k : k + 1])

        @pl.when(up_z)
        def _():
            start(f_zf[k : k + 1])

    forward(0)

    @pl.when(z > 0)
    def _():
        round_yx()


    @pl.when(core == 1)
    def _():
        landed(f_z2)
        start_choice(f_c1b, 1)

    landed(f_c1a, f_c1b)
    tile(OWN * B, 4 * B, T1A, 2)
    landed(f_x2t, f_x2b)
    start(f_yx2y)
    forward(1)
    start(f_c3f)
    landed(f_yxp[1:], f_yxm[:1], f_c3f)
    tile(OWN * B, 4 * B, T2F, 2)
    tile(YXM * B, 2 * B, T0B, 6)
    def stage(row, rows):
        sp[pl.ds(row, rows), :] = pg[pl.ds(row, rows), :].astype(jnp.bfloat16)

    def stage_sum(row, at, rows):
        total = pg[pl.ds(row, rows), :] + rxh[pl.ds(at, rows), :].astype(jnp.float32)
        sp[pl.ds(row, rows), :] = total.astype(jnp.bfloat16)

    def text_sum(slot, k=0, rows=B):
        return tgr[pl.ds(slot * B + k * HALF, rows), :]

    def put(slot, value, k=0):
        sg[pl.ds(slot * B + k * HALF, value.shape[0]), :] = value.astype(jnp.bfloat16)

    def got(slot, k=0, rows=B):
        return rg[pl.ds(slot * B + k * HALF, rows), :].astype(jnp.float32)

    def last_texts():
        for k in range(2):

            @pl.when(from_below)
            def _():
                landed(f_zf[k : k + 1])

            @pl.when(jnp.logical_not(from_below))
            def _():
                landed(f_p2l[k : k + 1])

            start(f_c3l[k : k + 1])

    def ready_texts():
        put(G1A, text_sum(T1A))
        put(G1B, text_sum(T1B))
        start(b_c1)
        put(G3F, text_sum(T3F))
        start(b_c3f)

    def far_images():
        stage(YX2 * B, B)
        start(b_7t, b_7b, b_7y)

    def far_texts():
        for k in range(2):
            put(G3L, text_sum(T3L, k, HALF), k)
            start(b_c3l[k : k + 1])

    @pl.when(z == 0)
    def _():
        landed(f_yx2t, f_yx2b, f_yx2y)
        tile(X2 * B, 2 * B, T0B, 6)
        last_texts()
        ready_texts()
        landed(f_c3l)
        tile(X2 * B, 2 * B, T2L, 2)
        far_images()
        tile(YXM * B, 2 * B, T2L, 2)
        tile(OWN * B, 4 * B, T2L, 2)
        far_texts()

    @pl.when(z > 0)
    def _():
        last_texts()
        landed(f_c3l)
        tile(OWN * B, 4 * B, T2L, 2)
        landed(f_yx2t, f_yx2b, f_yx2y)
        tile(X2 * B, 2 * B, T0B, 8)
        far_images()
        tile(YXM * B, 2 * B, T2L, 2)
        far_texts()
        ready_texts()

    stage(YXM * B + QUARTER, 3 * QUARTER)
    start(b_4)
    stage(YXP * B, 3 * QUARTER)
    start(b_5)
    for k in range(2):
        landed(b_c3l[k : k + 1])
        put(G2L, text_sum(T2L, k, HALF) + got(G3L, k, HALF), k)
        start(b_zf[k : k + 1])
    landed(b_c1)

    @pl.when(core == 1)
    def _():
        start(b_zr)

    landed(b_7t)
    stage_sum(YXM * B, 0, QUARTER)
    start(b_4s)
    landed(b_7b)
    stage_sum(YXP * B + 3 * QUARTER, 3 * QUARTER, QUARTER)
    start(b_5s)
    landed(b_7y)
    stage(X2 * B, QUARTER)
    stage_sum(X2 * B + QUARTER, QUARTER, HALF)
    stage(X2 * B + 3 * QUARTER, QUARTER)
    start(b_6t, b_6b)

    sl[pl.ds(0, 8), :] = loss[...]
    start(l_c)
    stage(XM * B + HALF, HALF)
    start(b_1[1:])
    stage(XP * B, HALF)
    start(b_2[:1])
    landed(b_c3f, l_c)
    loss_2f = loss[pl.ds(T2F, 1), :] + rl[pl.ds(T3F, 1), :]
    loss_2l = loss[pl.ds(T2L, 1), :] + rl[pl.ds(T3L, 1), :]
    sl[pl.ds(8, 8), :] = jnp.broadcast_to(loss_2l, (8, B))
    start(l_zf)

    @pl.when(core == 1)
    def _():
        start(l_zr)

    for k in range(2):
        landed(b_zf[k : k + 1])
        total = text_sum(T2F, k, HALF) + got(G3F, k, HALF) + got(G2L, k, HALF)
        put(G2F, total, k)
        start(b_p2f[k : k + 1])
    landed(l_zf)
    sl[pl.ds(16, 8), :] = jnp.broadcast_to(loss_2f + rl[pl.ds(8, 1), :], (8, B))
    start(l_p)

    tgr[pl.ds(T0A * B, B), :] += got(G1A)
    loss[pl.ds(T0A, 1), :] += rl[pl.ds(T1A, 1), :]

    @pl.when(core == 1)
    def _():
        landed(b_zr, l_zr)
        tgr[pl.ds(T0A * B, B), :] += got(GR)
        loss[pl.ds(T0A, 1), :] += rl[pl.ds(24 + T1B, 1), :]

    def down_z(k, add):
        value = text_sum(T0A, k, HALF)
        if add:
            value += got(G2F, k, HALF)
        put(GS, value, k)
        start(b_zs[k : k + 1])

    @pl.when(y_lo == 0)
    def _():
        down_z(0, False)
        down_z(1, False)

    landed(b_6t)
    stage_sum(XM * B, B, HALF)
    start(b_1[:1])
    landed(b_6b)
    stage_sum(XP * B + HALF, B + HALF, HALF)
    start(b_2[1:])

    @pl.when(y_lo == 1)
    def _():
        landed(b_p2f[:1])
        down_z(0, True)

    landed(b_4, b_5, b_4s, b_5s)
    for k in range(2):
        total = (
            pg[pl.ds(Y * B + k * HALF, HALF), :]
            + rx[pl.ds(0 * B + k * HALF, HALF), :].astype(jnp.float32)
            + rx[pl.ds(1 * B + k * HALF, HALF), :].astype(jnp.float32)
        )
        sp[pl.ds(Y * B + k * HALF, HALF), :] = total.astype(jnp.bfloat16)
        start(b_3[k : k + 1])

    landed(l_p)

    @pl.when(y_lo == 1)
    def _():
        landed(b_p2f[1:])
        down_z(1, True)
        loss[pl.ds(T0A, 1), :] += rl[pl.ds(16, 1), :]

    sl[pl.ds(24, 8), :] = jnp.broadcast_to(loss[pl.ds(T0A, 1), :], (8, B))
    start(l_zs)

    @pl.when(y_lo == 0)
    def _():
        landed(b_p2f)
        tgr[pl.ds(T0B * B, B), :] += got(G2F)
        loss[pl.ds(T0B, 1), :] += rl[pl.ds(16, 1), :]

    @pl.when(core == 0)
    def _():
        tgr[pl.ds(T0B * B, B), :] += got(G1B)
        loss[pl.ds(T0B, 1), :] += rl[pl.ds(T1B, 1), :]

    wide_temper = jnp.concatenate([temper] * (images.shape[1] // B), axis=1)

    landed(b_1, b_2, b_3)
    image_sum = (
        pg[pl.ds(OWN * B, B), :]
        + rx[pl.ds(2 * B, B), :].astype(jnp.float32)
        + rx[pl.ds(3 * B, B), :].astype(jnp.float32)
        + rx[pl.ds(4 * B, B), :].astype(jnp.float32)
    )
    unit, inverse = normalized(images)
    image_grad[...] = chain_back(unit, inverse, wide_temper * image_sum)

    landed(b_zs, l_zs)
    unit, inverse = normalized(texts)
    text_grad[...] = chain_back(unit, inverse, wide_temper * (text_sum(T0B) + got(GS)))
    text_loss[...] = (loss[pl.ds(T0B, 1), :] + rl[pl.ds(32, 1), :]) * (1.0 / STEPS)

    left(f_xp, f_xm, f_y, f_x2t, f_x2b, f_yxp, f_yxm, f_yx2t, f_yx2b, f_yx2y)
    left(f_z1, f_c1a, f_c1b, f_p2f, f_c3f, f_c3l)
    left(b_7t, b_7b, b_7y, b_6t, b_6b, b_4, b_5, b_4s, b_5s, b_1, b_2, b_3)
    left(b_c3l, b_c3f, b_c1, b_p2f, b_zf, b_zs, l_c, l_p, l_zf, l_zs)

    @pl.when(core == 1)
    def _():
        left(f_z2, b_zr, l_zr)

    @pl.when(up_z)
    def _():
        left(f_zf)

    @pl.when(jnp.logical_and(z == 0, y_lo == 0))
    def _():
        left(f_p2l)


SEMS = 80


def on_device(images, texts, log_scale, bias):
    width = images.shape[1]
    images = pltpu.with_memory_space_constraint(images, pltpu.HBM)
    texts = pltpu.with_memory_space_constraint(texts, pltpu.HBM)
    rows = lambda n, dtype: pltpu.VMEM((n, width), dtype)
    vmem = pl.BlockSpec(memory_space=pltpu.VMEM)
    smem = pl.BlockSpec(memory_space=pltpu.SMEM)
    hbm = pl.BlockSpec(memory_space=pltpu.HBM)
    image_grad, text_grad, text_loss = pl.pallas_call(
        kernel,
        out_shape=(
            jax.ShapeDtypeStruct((B, width), jnp.float32),
            jax.ShapeDtypeStruct((B, width), jnp.float32),
            jax.ShapeDtypeStruct((1, B), jnp.float32),
        ),
        in_specs=[hbm, hbm, smem, smem],
        out_specs=(vmem, vmem, vmem),
        scratch_shapes=[
            rows(B, jnp.bfloat16),
            rows(B, jnp.bfloat16),
            rows(8 * B, jnp.bfloat16),
            rows(9 * B, jnp.bfloat16),
            rows(8 * B, jnp.float32),
            rows(8 * B, jnp.float32),
            pltpu.VMEM((8, B), jnp.float32),
            rows(8 * B, jnp.bfloat16),
            rows(4 * HALF, jnp.bfloat16),
            rows(5 * B, jnp.bfloat16),
            rows(8 * B, jnp.bfloat16),
            rows(8 * B, jnp.bfloat16),
            pltpu.VMEM((32, B), jnp.float32),
            pltpu.VMEM((40, B), jnp.float32),
            pltpu.SemaphoreType.DMA((2,)),
            pltpu.SemaphoreType.DMA((SEMS,)),
            pltpu.SemaphoreType.DMA((SEMS,)),
        ],
        compiler_params=pltpu.CompilerParams(
            collective_id=0, has_side_effects=True, vmem_limit_bytes=52 << 20
        ),
        name="window",
    )(images, texts, log_scale, bias)
    return image_grad, text_grad, text_loss.reshape(B)


def solution(mesh):
    return jax.shard_map(
        on_device,
        mesh=mesh,
        in_specs=(P(("blk", "member"), None), P(("blk", "member"), None), P(), P()),
        out_specs=(P(("blk", "member"), None), P(("blk", "member"), None), P(("blk", "member"))),
        check_vma=False,
    )
```

```python
import jax
import jax.numpy as jnp
from jax import lax
from jax.experimental import pallas as pl
from jax.experimental.pallas import tpu as pltpu
from jax.sharding import PartitionSpec as P

STEPS = 8
B = 128
HALF = B // 2
QUARTER = B // 4
MESH = pl.DeviceIdType.MESH

OWN, XM, XP, Y, YXM, YXP, X2, YX2 = range(8)
T0B, T0A, T1A, T1B, T2F, T3F, T2L, T3L, RELAY = range(9)
G1A, G1B, G2F, G2L, G3F, G3L, GR, GS = range(8)


def normalized(values):
    wide = values.astype(jnp.float32)
    inverse = lax.rsqrt(jnp.sum(wide * wide, axis=-1, keepdims=True) + 1e-06)
    return wide * inverse, inverse


def chain_back(unit, inverse, upstream):
    return inverse * (upstream - unit * jnp.sum(unit * upstream, axis=-1, keepdims=True))


def kernel(
    images_in, texts_in, log_scale, bias, image_grad, text_grad, text_loss,
    images, texts, img, txt, kept, pg, tgr, loss, sp, rxh, rx, sg, rg, sl, rl, isem, ssem, rsem,
):
    blk, member = lax.axis_index("blk"), lax.axis_index("member")
    n_blk, n_member = lax.axis_size("blk"), lax.axis_size("member")
    core = blk % 2
    y_lo = (blk // 2) % 2
    z = blk // 4
    at_core = (blk + 1 - 2 * core, member)
    at_pair = (blk + 2 - 4 * y_lo, member)
    at_zp = ((blk + 4) % n_blk, member)
    at_zm = ((blk + n_blk - 4) % n_blk, member)
    at_xp = (blk, (member + 2) % n_member)
    at_xm = (blk, (member + n_member - 2) % n_member)
    at_y = (blk, member + 1 - 2 * (member % 2))

    image_load = pltpu.make_async_copy(images_in, images, isem.at[0])
    text_load = pltpu.make_async_copy(texts_in, texts, isem.at[1])
    image_load.start()
    text_load.start()

    barrier = pltpu.get_barrier_semaphore()
    partners = (at_core, at_pair, at_zm, at_xp, at_xm, at_y)
    for device in partners:
        pl.semaphore_signal(barrier, inc=1, device_id=device, device_id_type=MESH)

    used = [0]

    def copies(src, src_row, dst, dst_row, rows, device, pieces=1, other=None):
        out = []
        step = rows // pieces
        for k in range(pieces):
            s = used[0]
            used[0] += 1
            made = [
                pltpu.make_async_remote_copy(
                    src_ref=a.at[pl.ds(r + k * step, step)],
                    dst_ref=dst.at[pl.ds(dst_row + k * step, step)],
                    send_sem=ssem.at[s],
                    recv_sem=rsem.at[s],
                    device_id=device,
                    device_id_type=MESH,
                )
                for a, r in [(src, src_row)] + ([other] if other else [])
            ]
            out.append(made if other else made[0])
        return out

    f_xp = copies(img, OWN * B, img, XM * B, B, at_xp, 2)
    f_xm = copies(img, OWN * B, img, XP * B, B, at_xm, 2)
    outer = (0, 3 * QUARTER)
    f_yo = [c for r in outer for c in copies(img, OWN * B + r, img, Y * B + r, QUARTER, at_y)]
    f_ym = copies(img, OWN * B + QUARTER, img, Y * B + QUARTER, HALF, at_y)
    f_x2t = copies(img, XM * B, img, X2 * B, HALF, at_xp)
    f_x2b = copies(img, XP * B + HALF, img, X2 * B + HALF, HALF, at_xm)
    f_yxpo = [c for r in outer for c in copies(img, Y * B + r, img, YXM * B + r, QUARTER, at_xp)]
    f_yxmo = [c for r in outer for c in copies(img, Y * B + r, img, YXP * B + r, QUARTER, at_xm)]
    f_yxp = copies(img, Y * B + QUARTER, img, YXM * B + QUARTER, HALF, at_xp)
    f_yxm = copies(img, Y * B + QUARTER, img, YXP * B + QUARTER, HALF, at_xm)
    f_yx2t = copies(img, YXM * B, img, YX2 * B, QUARTER, at_xp)
    f_yx2b = copies(img, YXP * B + 3 * QUARTER, img, YX2 * B + 3 * QUARTER, QUARTER, at_xm)
    f_yx2y = copies(img, X2 * B + QUARTER, img, YX2 * B + QUARTER, HALF, at_y)
    f_z1 = copies(txt, T0B * B, txt, T0A * B, B, at_zp, 2)
    f_c1a = copies(txt, T0A * B, txt, T1A * B, B, at_core)
    f_z2 = copies(txt, T0A * B, txt, RELAY * B, B, at_zp, 2)
    f_c1b = copies(txt, T0B * B, txt, T1B * B, B, at_core, 1, (txt, RELAY * B))
    f_p2f = copies(txt, T0B * B, txt, T2F * B, B, at_pair, 2, (txt, T0A * B))
    f_p2l = copies(txt, T0A * B, txt, T2L * B, B, at_pair, 2)
    f_zf = copies(txt, T2F * B, txt, T2L * B, B, at_zp, 2)
    f_c3f = copies(txt, T2F * B, txt, T3F * B, B, at_core)
    f_c3l = copies(txt, T2L * B, txt, T3L * B, B, at_core, 2)
    b_7t = copies(sp, YX2 * B, rxh, 0, QUARTER, at_xm)
    b_7y = copies(sp, YX2 * B + QUARTER, rxh, QUARTER, HALF, at_y)
    b_7b = copies(sp, YX2 * B + 3 * QUARTER, rxh, 3 * QUARTER, QUARTER, at_xp)
    b_6t = copies(sp, X2 * B, rxh, B, HALF, at_xm)
    b_6b = copies(sp, X2 * B + HALF, rxh, B + HALF, HALF, at_xp)
    b_4s = copies(sp, YXM * B, rx, 0, QUARTER, at_xm)
    b_4 = copies(sp, YXM * B + QUARTER, rx, QUARTER, 3 * QUARTER, at_xm)
    b_5 = copies(sp, YXP * B, rx, B, 3 * QUARTER, at_xp)
    b_5s = copies(sp, YXP * B + 3 * QUARTER, rx, B + 3 * QUARTER, QUARTER, at_xp)
    b_1 = copies(sp, XM * B, rx, 2 * B, B, at_xm, 2)
    b_2 = copies(sp, XP * B, rx, 3 * B, B, at_xp, 2)
    b_3 = copies(sp, Y * B, rx, 4 * B, B, at_y, 2)
    b_c3l = copies(sg, G3L * B, rg, G3L * B, B, at_core, 2)
    b_c3f = copies(sg, G3F * B, rg, G3F * B, B, at_core)
    b_c1 = copies(sg, G1A * B, rg, G1A * B, 2 * B, at_core)
    b_zf = copies(sg, G2L * B, rg, G2L * B, B, at_zm, 2)
    b_p2f = copies(sg, G2F * B, rg, G2F * B, B, at_pair, 2)
    b_zr = copies(rg, G1B * B, rg, GR * B, B, at_zm, 2)
    b_zs = copies(sg, GS * B, rg, GS * B, B, at_zm, 2)
    l_c = copies(sl, 0, rl, 0, 8, at_core)
    l_zf = copies(sl, 8, rl, 8, 8, at_zm)
    l_p = copies(sl, 16, rl, 16, 8, at_pair)
    l_zr = copies(rl, 0, rl, 24, 8, at_zm)
    l_zs = copies(sl, 24, rl, 32, 8, at_zm)

    def start(*lists):
        for group in lists:
            for c in group:
                c.start()

    def landed(*lists):
        for group in lists:
            for c in group:
                (c[0] if isinstance(c, list) else c).wait_recv()

    def left(*lists):
        for group in lists:
            for c in group:
                (c[0] if isinstance(c, list) else c).wait_send()

    def start_choice(group, which):
        for c in group:
            c[which].start()

    temper = jnp.exp(jnp.full((1, B), log_scale[0], jnp.float32))
    offset = bias[0]

    text_load.wait()
    unit, _ = normalized(texts[...])
    txt[pl.ds(T0B * B, B), :] = unit.astype(jnp.bfloat16)

    pl.semaphore_wait(barrier, len(partners))

    start(f_z1)
    image_load.wait()
    unit, _ = normalized(images[...])
    img[pl.ds(OWN * B, B), :] = unit.astype(jnp.bfloat16)
    start(f_yo, f_ym, f_xp, f_xm)

    @pl.when(core == 0)
    def _():
        start_choice(f_c1b, 0)

    pg[...] = jnp.zeros_like(pg)
    tgr[...] = jnp.zeros_like(tgr)
    loss[...] = jnp.zeros_like(loss)

    def tile(row, rows, first, blocks, diagonal=False, keep=False):
        cols = blocks * B
        i = img[pl.ds(row, rows), :]
        t = txt[pl.ds(first * B, cols), :]
        scale = jnp.concatenate([temper] * blocks, axis=1)
        logits = (
            lax.dot_general(i, t, (((1,), (1,)), ((), ())), preferred_element_type=jnp.float32)
            * scale
            + offset
        )
        grown = jnp.exp(logits)
        slope = grown * pl.reciprocal(1.0 + grown, approx=True)
        part = rows
        while part > rows // 8:
            part //= 2
            grown = grown[:part] + grown[part:] + grown[:part] * grown[part:]
        logs = jnp.where(
            grown < 0.0078125,
            grown * (1.0 - grown * (0.5 - grown * (1.0 / 3.0))),
            jnp.log(1.0 + grown),
        )
        column = jnp.sum(logs, axis=0, keepdims=True)
        if diagonal:
            at_row = row + lax.broadcasted_iota(jnp.int32, (rows, cols), 0)
            at_col = first * B + lax.broadcasted_iota(jnp.int32, (rows, cols), 1)
            matched = jnp.logical_and(at_row == at_col, at_col < B)
            slope = slope - jnp.where(matched, 1.0, 0.0)
            column = column - jnp.sum(jnp.where(matched, logits, 0.0), axis=0, keepdims=True)
        for k in range(blocks):
            loss[pl.ds(first + k, 1), :] += column[:, k * B : (k + 1) * B]
        low = slope.astype(jnp.bfloat16)
        pg[pl.ds(row, rows), :] += jnp.dot(low, t, preferred_element_type=jnp.float32)
        if keep:
            kept[:, pl.ds(0, cols)] = low
        else:
            text_part(low, i, first, cols)

    def text_part(low, i, first, cols):
        tgr[pl.ds(first * B, cols), :] += lax.dot_general(
            low, i, (((0,), (0,)), ((), ())), preferred_element_type=jnp.float32
        )

    def from_z(k):
        landed(f_z1[k : k + 1])

        @pl.when(core == 1)
        def _():
            start(f_z2[k : k + 1])

        @pl.when(y_lo == 1)
        def _():
            start_choice(f_p2f[k : k + 1], 1)

    def from_y_outer():
        landed(f_yo)
        start(f_yxpo[:1], f_yxmo[1:], f_yxpo[1:], f_yxmo[:1])

    def from_y_middle():
        landed(f_ym)
        start(f_yxp, f_yxm)

        @pl.when(y_lo == 0)
        def _():
            start_choice(f_p2f, 0)

    def round_x():
        landed(f_xp, f_xm)
        start(f_x2t, f_x2b)

    def round_yx():
        landed(f_yxpo[:1])
        start(f_yx2t)
        landed(f_yxmo[1:])
        start(f_yx2b)

    @pl.when(z == 0)
    def _():
        from_y_outer()
        round_x()
        from_y_middle()
        round_yx()
        for k in range(2):
            from_z(k)

            @pl.when(y_lo == 0)
            def _():
                start(f_p2l[k : k + 1])

    @pl.when(z > 0)
    def _():
        from_z(0)
        from_y_outer()
        from_z(1)
        round_x()
        from_y_middle()

    start(f_c1a)
    tile(OWN * B, 4 * B, T0B, 2, diagonal=True)

    @pl.when(z > 0)
    def _():
        round_yx()

    up_z = jnp.logical_or(y_lo == 0, z < n_blk // 4 - 1)
    from_below = jnp.logical_or(y_lo == 0, z > 0)

    def forward(k):
        landed(f_p2f[k : k + 1])

        @pl.when(up_z)
        def _():
            start(f_zf[k : k + 1])

    forward(0)


    @pl.when(core == 1)
    def _():
        landed(f_z2)
        start_choice(f_c1b, 1)

    landed(f_c1a, f_c1b)
    tile(OWN * B, 4 * B, T1A, 2)
    landed(f_x2t, f_x2b)
    start(f_yx2y)
    forward(1)
    start(f_c3f)
    landed(f_yxpo[1:], f_yxmo[:1], f_yxp, f_yxm, f_c3f)
    tile(OWN * B, 4 * B, T2F, 2)
    tile(YXM * B, 2 * B, T0B, 6)
    def stage(row, rows):
        sp[pl.ds(row, rows), :] = pg[pl.ds(row, rows), :].astype(jnp.bfloat16)

    def stage_sum(row, at, rows):
        total = pg[pl.ds(row, rows), :] + rxh[pl.ds(at, rows), :].astype(jnp.float32)
        sp[pl.ds(row, rows), :] = total.astype(jnp.bfloat16)

    def text_sum(slot, k=0, rows=B):
        return tgr[pl.ds(slot * B + k * HALF, rows), :]

    def put(slot, value, k=0):
        sg[pl.ds(slot * B + k * HALF, value.shape[0]), :] = value.astype(jnp.bfloat16)

    def got(slot, k=0, rows=B):
        return rg[pl.ds(slot * B + k * HALF, rows), :].astype(jnp.float32)

    def last_texts():
        for k in range(2):

            @pl.when(from_below)
            def _():
                landed(f_zf[k : k + 1])

            @pl.when(jnp.logical_not(from_below))
            def _():
                landed(f_p2l[k : k + 1])

            start(f_c3l[k : k + 1])

    def ready_texts():
        put(G1A, text_sum(T1A))
        put(G1B, text_sum(T1B))
        start(b_c1)
        put(G3F, text_sum(T3F))
        start(b_c3f)

    def far_images():
        stage(YX2 * B, B)
        start(b_7t, b_7b, b_7y)

    def far_texts():
        for k in range(2):
            put(G3L, text_sum(T3L, k, HALF), k)
            start(b_c3l[k : k + 1])

    last_texts()
    landed(f_c3l)
    tile(OWN * B, 4 * B, T2L, 2)
    landed(f_yx2t, f_yx2b, f_yx2y)
    tile(X2 * B, 2 * B, T0B, 8, keep=True)
    far_images()
    text_part(kept[...], img[pl.ds(X2 * B, 2 * B), :], T0B, 8 * B)
    tile(YXM * B, 2 * B, T2L, 2)
    far_texts()
    ready_texts()

    stage(YXM * B + QUARTER, 3 * QUARTER)
    start(b_4)
    stage(YXP * B, 3 * QUARTER)
    start(b_5)
    for k in range(2):
        landed(b_c3l[k : k + 1])
        put(G2L, text_sum(T2L, k, HALF) + got(G3L, k, HALF), k)
        start(b_zf[k : k + 1])
    landed(b_c1)

    @pl.when(core == 1)
    def _():
        start(b_zr)

    landed(b_7t)
    stage_sum(YXM * B, 0, QUARTER)
    start(b_4s)
    landed(b_7b)
    stage_sum(YXP * B + 3 * QUARTER, 3 * QUARTER, QUARTER)
    start(b_5s)
    landed(b_7y)
    stage(X2 * B, QUARTER)
    stage_sum(X2 * B + QUARTER, QUARTER, HALF)
    stage(X2 * B + 3 * QUARTER, QUARTER)
    start(b_6t, b_6b)

    sl[pl.ds(0, 8), :] = loss[...]
    start(l_c)
    stage(XM * B + HALF, HALF)
    start(b_1[1:])
    stage(XP * B, HALF)
    start(b_2[:1])
    landed(b_c3f, l_c)
    loss_2f = loss[pl.ds(T2F, 1), :] + rl[pl.ds(T3F, 1), :]
    loss_2l = loss[pl.ds(T2L, 1), :] + rl[pl.ds(T3L, 1), :]
    sl[pl.ds(8, 8), :] = jnp.broadcast_to(loss_2l, (8, B))
    start(l_zf)

    @pl.when(core == 1)
    def _():
        start(l_zr)

    for k in range(2):
        landed(b_zf[k : k + 1])
        total = text_sum(T2F, k, HALF) + got(G3F, k, HALF) + got(G2L, k, HALF)
        put(G2F, total, k)
        start(b_p2f[k : k + 1])
    landed(l_zf)
    sl[pl.ds(16, 8), :] = jnp.broadcast_to(loss_2f + rl[pl.ds(8, 1), :], (8, B))
    start(l_p)

    tgr[pl.ds(T0A * B, B), :] += got(G1A)
    loss[pl.ds(T0A, 1), :] += rl[pl.ds(T1A, 1), :]

    @pl.when(core == 1)
    def _():
        landed(b_zr, l_zr)
        tgr[pl.ds(T0A * B, B), :] += got(GR)
        loss[pl.ds(T0A, 1), :] += rl[pl.ds(24 + T1B, 1), :]

    def down_z(k, add):
        value = text_sum(T0A, k, HALF)
        if add:
            value += got(G2F, k, HALF)
        put(GS, value, k)
        start(b_zs[k : k + 1])

    @pl.when(y_lo == 0)
    def _():
        down_z(0, False)
        down_z(1, False)

    landed(b_6t)
    stage_sum(XM * B, B, HALF)
    start(b_1[:1])
    landed(b_6b)
    stage_sum(XP * B + HALF, B + HALF, HALF)
    start(b_2[1:])

    @pl.when(y_lo == 1)
    def _():
        landed(b_p2f[:1])
        down_z(0, True)

    landed(b_4, b_5, b_4s, b_5s)
    for k in range(2):
        total = (
            pg[pl.ds(Y * B + k * HALF, HALF), :]
            + rx[pl.ds(0 * B + k * HALF, HALF), :].astype(jnp.float32)
            + rx[pl.ds(1 * B + k * HALF, HALF), :].astype(jnp.float32)
        )
        sp[pl.ds(Y * B + k * HALF, HALF), :] = total.astype(jnp.bfloat16)
        start(b_3[k : k + 1])

    landed(l_p)

    @pl.when(y_lo == 1)
    def _():
        landed(b_p2f[1:])
        down_z(1, True)
        loss[pl.ds(T0A, 1), :] += rl[pl.ds(16, 1), :]

    sl[pl.ds(24, 8), :] = jnp.broadcast_to(loss[pl.ds(T0A, 1), :], (8, B))
    start(l_zs)

    @pl.when(y_lo == 0)
    def _():
        landed(b_p2f)
        tgr[pl.ds(T0B * B, B), :] += got(G2F)
        loss[pl.ds(T0B, 1), :] += rl[pl.ds(16, 1), :]

    @pl.when(core == 0)
    def _():
        tgr[pl.ds(T0B * B, B), :] += got(G1B)
        loss[pl.ds(T0B, 1), :] += rl[pl.ds(T1B, 1), :]

    wide_temper = jnp.concatenate([temper] * (images.shape[1] // B), axis=1)

    landed(b_1, b_2)
    pg[pl.ds(OWN * B, B), :] += rx[pl.ds(2 * B, B), :].astype(jnp.float32) + rx[
        pl.ds(3 * B, B), :
    ].astype(jnp.float32)
    for k in range(2):
        part = pl.ds(k * HALF, HALF)
        landed(b_3[k : k + 1])
        image_sum = pg[pl.ds(OWN * B + k * HALF, HALF), :] + rx[
            pl.ds(4 * B + k * HALF, HALF), :
        ].astype(jnp.float32)
        unit, inverse = normalized(images[part, :])
        image_grad[part, :] = chain_back(unit, inverse, wide_temper * image_sum)
    for k in range(2):
        part = pl.ds(k * HALF, HALF)
        landed(b_zs[k : k + 1])
        unit, inverse = normalized(texts[part, :])
        total = text_sum(T0B, k, HALF) + got(GS, k, HALF)
        text_grad[part, :] = chain_back(unit, inverse, wide_temper * total)
    landed(l_zs)
    text_loss[...] = (loss[pl.ds(T0B, 1), :] + rl[pl.ds(32, 1), :]) * (1.0 / STEPS)

    left(f_xp, f_xm, f_yo, f_ym, f_x2t, f_x2b, f_yxpo, f_yxmo, f_yxp, f_yxm, f_yx2t, f_yx2b, f_yx2y)
    left(f_z1, f_c1a, f_c1b, f_p2f, f_c3f, f_c3l)
    left(b_7t, b_7b, b_7y, b_6t, b_6b, b_4, b_5, b_4s, b_5s, b_1, b_2, b_3)
    left(b_c3l, b_c3f, b_c1, b_p2f, b_zf, b_zs, l_c, l_p, l_zf, l_zs)

    @pl.when(core == 1)
    def _():
        left(f_z2, b_zr, l_zr)

    @pl.when(up_z)
    def _():
        left(f_zf)

    @pl.when(jnp.logical_and(z == 0, y_lo == 0))
    def _():
        left(f_p2l)


SEMS = 80


def on_device(images, texts, log_scale, bias):
    width = images.shape[1]
    images = pltpu.with_memory_space_constraint(images, pltpu.HBM)
    texts = pltpu.with_memory_space_constraint(texts, pltpu.HBM)
    rows = lambda n, dtype: pltpu.VMEM((n, width), dtype)
    vmem = pl.BlockSpec(memory_space=pltpu.VMEM)
    smem = pl.BlockSpec(memory_space=pltpu.SMEM)
    hbm = pl.BlockSpec(memory_space=pltpu.HBM)
    image_grad, text_grad, text_loss = pl.pallas_call(
        kernel,
        out_shape=(
            jax.ShapeDtypeStruct((B, width), jnp.float32),
            jax.ShapeDtypeStruct((B, width), jnp.float32),
            jax.ShapeDtypeStruct((1, B), jnp.float32),
        ),
        in_specs=[hbm, hbm, smem, smem],
        out_specs=(vmem, vmem, vmem),
        scratch_shapes=[
            rows(B, jnp.bfloat16),
            rows(B, jnp.bfloat16),
            rows(8 * B, jnp.bfloat16),
            rows(9 * B, jnp.bfloat16),
            pltpu.VMEM((2 * B, 8 * B), jnp.bfloat16),
            rows(8 * B, jnp.float32),
            rows(8 * B, jnp.float32),
            pltpu.VMEM((8, B), jnp.float32),
            rows(8 * B, jnp.bfloat16),
            rows(4 * HALF, jnp.bfloat16),
            rows(5 * B, jnp.bfloat16),
            rows(8 * B, jnp.bfloat16),
            rows(8 * B, jnp.bfloat16),
            pltpu.VMEM((32, B), jnp.float32),
            pltpu.VMEM((40, B), jnp.float32),
            pltpu.SemaphoreType.DMA((2,)),
            pltpu.SemaphoreType.DMA((SEMS,)),
            pltpu.SemaphoreType.DMA((SEMS,)),
        ],
        compiler_params=pltpu.CompilerParams(
            collective_id=0, has_side_effects=True, vmem_limit_bytes=52 << 20
        ),
        name="window",
    )(images, texts, log_scale, bias)
    return image_grad, text_grad, text_loss.reshape(B)


def solution(mesh):
    return jax.shard_map(
        on_device,
        mesh=mesh,
        in_specs=(P(("blk", "member"), None), P(("blk", "member"), None), P(), P()),
        out_specs=(P(("blk", "member"), None), P(("blk", "member"), None), P(("blk", "member"))),
        check_vma=False,
    )
```
